256 devices in a mesh: dp: 64 (over y_lo, z, x), mp: 4 (over y_hi, core).
Axes of the slice: x: 4, y: 4 (y_hi: 2, y_lo: 2; y = y_hi * 2 + y_lo), z: 8, core: 2. Of those that a mesh axis runs over, the one named last changes fastest.
Arguments:
- tokens: bfloat16 [8192, 3584], P('dp', 'mp'), may hold values from -6 to 6
- routes: int32 [8192, 2], P('dp'), may hold values from 0 to 63, all different within a row; in each aligned block of 128 rows (0 to 127, 128 to 255, ...) at most 5 rows name the same one
- expert_gate_affinity: float32 [8192, 2], P('dp'), may hold values from 0.05 to 1
- expert_gate_weight: bfloat16 [64, 3584, 2048], P('dp', None, 'mp'), may hold values from -0.09375 to 0.09375
- expert_up_weight: bfloat16 [64, 3584, 2048], P('dp', None, 'mp'), may hold values from -0.09375 to 0.09375
- expert_down_weight: bfloat16 [64, 2048, 3584], P('dp', 'mp'), may hold values from -0.125 to 0.125
- proj: bfloat16 [3584, 5120], P('dp', 'mp'), may hold values from -0.09375 to 0.09375
- student_hidden_input: bfloat16 [8192, 5120], P('dp', 'mp'), may hold values from -6 to 6
- student_norm_weight: bfloat16 [5120], P('mp'), may hold values from 0.25 to 1.75
- adapter_down_matrix: bfloat16 [5120, 64], P('mp'), may hold values from -0.078125 to 0.078125
- adapter_up_matrix: bfloat16 [64, 5120], P(None, 'mp'), may hold values from -0.75 to 0.75
Outputs:
- target: float32 [8192, 5120], P('dp', 'mp')
- grad_a: float32 [5120, 64], P('mp')
- up_matrix_gradient: float32 [64, 5120], P(None, 'mp')
- loss: float32 [], replicated
The draws below stay inside these ranges and needn't reach their ends.
Inputs may be any that keep to these rules, and one draw needn't show every extreme that they name: `routes`: each row names 2 different experts; within the 128 rows of one index of dp no expert is named more than 5 times, and in every draw some index of dp names some expert exactly 5 times.
All inputs are finite; a program needn't handle non-finite values.
Results may differ from the reference program's by a relative error of at most 0.018.
Values may be sent and summed in bfloat16 or wider, within the bound.
No kernel may reach another device: no remote copies, remote signals or barrier semaphores. Data moves between devices by JAX's collectives and lax.ppermute only.
A program may use at most 128 MiB of HBM per device.

```python
import math
import jax
import jax.numpy as jnp
import numpy as np
from jax import lax

D = 3584
FFT = 2048
STUDENT_DIM = 5120
ADAPTER_RANK = 64
TOPK = 2
TD = 128
EXPERTS = 64
CAP = 5
TOKENS = 8192
N_DP = 64
N_MP = 4


def level_of(rng, shape, split, low, top_value):
    def one(dim, parts):
        draws = jax.random.uniform(jax.random.fold_in(jax.random.fold_in(rng, 6), dim), (parts,), jnp.float32, low / len(split), top_value / len(split))
        return jnp.repeat(jnp.exp(draws), shape[dim] // parts).reshape((-1,) + (1,) * (len(shape) - dim - 1))

    loudness = one(*split[0])
    for cut in split[1:]:
        loudness = loudness * one(*cut)
    return loudness


def assign_block(rng, own, number, rows, count, top, reach, slope):
    ranking = jax.random.permutation(rng, count)
    crowded, usual = load_shares(count, rows * top, reach, slope, True), load_shares(count, rows * top, reach, slope, False)
    places = jnp.arange(count)

    def named(sizes, rotation):
        used = int((sizes > 0).sum())
        fixed = max(1, used // 4)
        passed = fixed + (places - fixed + rotation * (used - fixed)) % max(1, count - fixed)
        return jnp.zeros((count,), jnp.int32).at[ranking[jnp.where(places < fixed, places, passed)]].set(jnp.asarray(sizes, jnp.int32))

    sizes = jnp.where(number % 4 == 0, named(crowded, number // 4), named(usual, number - number // 4 - 1))
    mixed = jax.random.permutation(jax.random.fold_in(own, 3), count)
    giver, taker = mixed[0:count // 2 * 2:2], mixed[1:count // 2 * 2:2]
    room = jnp.minimum(sizes[giver] - 1, reach - sizes[taker]) // 2
    room = jnp.where((giver == ranking[0]) | (taker == ranking[0]) | (sizes[taker] == 0), 0, jnp.maximum(room, 0))
    passed = jax.random.randint(jax.random.fold_in(own, 4), (count // 2,), 0, 1 << 20) % (room + 1)
    sizes = sizes.at[giver].add(-passed).at[taker].add(passed)
    members = jnp.searchsorted(jnp.cumsum(sizes), jnp.arange(rows * top), side="right").astype(jnp.int32)
    grid = members.reshape(top, rows).T
    grid = grid[jax.random.permutation(jax.random.fold_in(own, 1), rows)]
    rotation = jax.random.randint(jax.random.fold_in(own, 2), (rows, 1), 0, top)
    return jnp.take_along_axis(grid, (jnp.arange(top)[None, :] + rotation) % top, axis=1)


def load_shares(number_of, total, most, lean, full):
    portions = [(1 << 20) // math.isqrt(standing ** lean) + 1 for standing in range(1, number_of + 1)]
    largest = most if full else min(most, max(-(-total // number_of), total * portions[0] // sum(portions)))
    least = 1 if total - largest >= number_of - 1 else 0
    counts, rest = [largest] + [least] * (number_of - 1), total - largest - least * (number_of - 1)
    while rest > 0:
        free = [i for i in range(1, number_of) if counts[i] < largest] or [i for i in range(1, number_of) if counts[i] < most]
        mass, remaining = sum([portions[i] for i in free]), rest
        for i in free:
            more = min(most - counts[i], max(1, remaining * portions[i] // mass), rest)
            counts[i] = counts[i] + more
            rest = rest - more
    return np.array(counts)


def scatter_about(stream_key, shape, scale, reach, pieces=(), held_as=jnp.bfloat16):
    entries = scale * jax.random.normal(stream_key, shape, jnp.float32)
    if pieces:
        entries = entries * level_of(stream_key, shape, pieces, -0.22, 0.18)
    return jnp.clip(entries, -reach, reach).astype(held_as)


def setup_inputs(seed: int = 0) -> dict:
    splits = jax.random.split(jax.random.key(seed), 12)
    tokens = scatter_about(splits[0], (TOKENS, D), 1.0, 6.0, ((0, 64), (1, 4)))
    routes_keys = jax.random.split(jax.random.fold_in(splits[1], 1), TOKENS // TD)
    routes_turns = jax.random.permutation(jax.random.fold_in(splits[1], 3), TOKENS // TD)
    routes = jax.vmap(lambda own, number: assign_block(jax.random.fold_in(splits[1], 2), own, number, TD, N_DP, TOPK, CAP, 2))(routes_keys, routes_turns).reshape((TOKENS, TOPK))
    expert_gate_affinity = jnp.clip(jnp.exp(math.log(1.0) - 2.9957323 * jax.random.uniform(splits[2], (TOKENS, TOPK), jnp.float32) ** level_of(splits[2], (TOKENS, TOPK), ((0, 64),), -0.2, 0.2)), 0.05, 1.0)
    expert_gate_weight = scatter_about(splits[3], (EXPERTS, D, FFT), D ** -0.5, 0.09375, ((0, 64), (2, 4)))
    expert_up_weight = scatter_about(splits[4], (EXPERTS, D, FFT), D ** -0.5, 0.09375, ((0, 64), (2, 4)))
    expert_down_weight = scatter_about(splits[5], (EXPERTS, FFT, D), FFT ** -0.5, 0.125, ((0, 64), (1, 4)))
    proj = scatter_about(splits[6], (D, STUDENT_DIM), D ** -0.5, 0.09375, ((0, 64), (1, 4)))
    student_hidden_input = scatter_about(splits[7], (TOKENS, STUDENT_DIM), 1.0, 6.0, ((0, 64), (1, 4)))
    student_norm_weight = jnp.clip(1.0 + 0.15 * jax.random.normal(splits[8], (STUDENT_DIM,), jnp.float32), 0.25, 1.75).astype(jnp.bfloat16)
    adapter_down_matrix = scatter_about(splits[9], (STUDENT_DIM, ADAPTER_RANK), STUDENT_DIM ** -0.5, 0.078125, ((0, 4),))
    adapter_up_matrix = scatter_about(splits[10], (ADAPTER_RANK, STUDENT_DIM), ADAPTER_RANK ** -0.5, 0.75, ((1, 4),))
    return {"tokens": tokens, "routes": routes, "expert_gate_affinity": expert_gate_affinity, "expert_gate_weight": expert_gate_weight, "expert_up_weight": expert_up_weight, "expert_down_weight": expert_down_weight, "proj": proj, "student_hidden_input": student_hidden_input, "student_norm_weight": student_norm_weight, "adapter_down_matrix": adapter_down_matrix, "adapter_up_matrix": adapter_up_matrix}


route_scale = 2.5
adapter_scale_factor = 0.25

def slot_tables(routes, expert_gate_affinity):
    per_block = TD * TOPK
    blocks = routes.reshape(N_DP, per_block).astype(jnp.int32)
    onehot_e = (blocks[:, :, None] == jnp.arange(N_DP, dtype=jnp.int32)[None, None, :]).astype(jnp.int32)
    position = lax.optimization_barrier(jnp.sum((jnp.cumsum(onehot_e, axis=1) - onehot_e) * onehot_e, axis=-1)).astype(jnp.int32)
    block_ids = jnp.arange(N_DP, dtype=jnp.int32)
    owner_row = (block_ids[:, None] * CAP + position).astype(jnp.int32)
    token_ids = (block_ids[:, None] * TD + jnp.arange(per_block, dtype=jnp.int32)[None, :] // TOPK).astype(jnp.int32)
    weights = route_scale * expert_gate_affinity / lax.optimization_barrier(jnp.sum(expert_gate_affinity, axis=-1, keepdims=True))
    slots_all = N_DP * CAP
    token_table = jnp.zeros((N_DP, slots_all), jnp.int32).at[blocks, owner_row].set(token_ids)
    weight_table = jnp.zeros((N_DP, slots_all), expert_gate_affinity.dtype).at[blocks, owner_row].set(weights.reshape(N_DP, per_block))
    return (token_table, weight_table)

def reference(tokens, routes, expert_gate_affinity, expert_gate_weight, expert_up_weight, expert_down_weight, proj, student_hidden_input, student_norm_weight, adapter_down_matrix, adapter_up_matrix):
    token_table, weight_table = slot_tables(routes, expert_gate_affinity)
    quarter = FFT // N_MP

    def expert_step(accum, expert):
        picked = jnp.take(tokens, token_table[expert], axis=0)
        gate_proj = jnp.dot(picked, expert_gate_weight[expert], preferred_element_type=jnp.float32)
        up_proj = jnp.dot(picked, expert_up_weight[expert], preferred_element_type=jnp.float32)
        hidden = (jax.nn.silu(gate_proj) * up_proj).astype(jnp.bfloat16)
        partial_sum = jnp.zeros((picked.shape[0], D), jnp.float32)
        for group in range(N_MP):
            term = jnp.dot(hidden[:, group * quarter:(group + 1) * quarter], expert_down_weight[expert, group * quarter:(group + 1) * quarter], preferred_element_type=jnp.float32)
            partial_sum = partial_sum + lax.optimization_barrier(term.astype(jnp.bfloat16)).astype(jnp.float32)
        expert_out = lax.optimization_barrier(partial_sum.astype(jnp.bfloat16)).astype(jnp.float32)
        accum = accum.at[token_table[expert]].add(weight_table[expert][:, None] * expert_out)
        return (accum, None)
    accum, _ = lax.scan(expert_step, jnp.zeros((TOKENS, D), jnp.float32), jnp.arange(N_DP, dtype=jnp.int32))
    teacher = accum.astype(jnp.bfloat16)
    target = jnp.dot(teacher, proj, preferred_element_type=jnp.float32)
    student_full_width = student_hidden_input.astype(jnp.float32)
    mean_sq = lax.optimization_barrier(jnp.mean(student_full_width * student_full_width, axis=-1, keepdims=True))
    normalized_states = (student_full_width * lax.rsqrt(mean_sq + 1e-06) * student_norm_weight.astype(jnp.float32)).astype(jnp.bfloat16)
    lowrank_product = jnp.dot(normalized_states, adapter_down_matrix, preferred_element_type=jnp.float32).astype(jnp.bfloat16)
    output_change = jnp.dot(lowrank_product, adapter_up_matrix, preferred_element_type=jnp.float32)
    output_difference = student_full_width + adapter_scale_factor * output_change - target
    loss = jnp.mean(output_difference * output_difference)
    scaled_states = (output_difference * (1.0 / math.sqrt(TOKENS))).astype(jnp.bfloat16)
    up_matrix_gradient = adapter_scale_factor * jnp.dot(lowrank_product.T, scaled_states, preferred_element_type=jnp.float32)
    backward_lowrank = (adapter_scale_factor * jnp.dot(scaled_states, adapter_up_matrix.T, preferred_element_type=jnp.float32)).astype(jnp.bfloat16)
    grad_a = jnp.dot(normalized_states.T, backward_lowrank, preferred_element_type=jnp.float32)
    return (target, grad_a, up_matrix_gradient, loss)
```

```python
import math

import jax
import jax.numpy as jnp
from jax import lax
from jax.sharding import Mesh, PartitionSpec as P

route_scale = 2.5
adapter_scale_factor = 0.25
DP = ("yl", "z", "x")
MP = ("yh", "c")
ALL = DP + MP
SIZES = (2, 8, 4, 2, 2)


def index_of(yl, z, x, yh, c):
    return (((yl * 8 + z) * 4 + x) * 2 + yh) * 2 + c


def coords():
    for yl in range(2):
        for z in range(8):
            for x in range(4):
                for yh in range(2):
                    for c in range(2):
                        yield yl, z, x, yh, c


def proj_perm():
    pairs = []
    for yl, z, x, yh, c in coords():
        d, m = (yl * 8 + z) * 4 + x, yh * 2 + c
        owner, place = d // 16, d % 16
        pairs.append(
            (index_of(yl, z, x, yh, c), index_of(place // 8, place % 8, m, owner // 2, owner % 2))
        )
    return pairs


def home_perm(step):
    pairs = []
    for yl, z, x, yh, c in coords():
        m = yh * 2 + c
        pairs.append(
            (index_of(yl, z, x, yh, c), index_of(yl, z, (x + m + step) % 4, x // 2, x % 2))
        )
    return pairs


def swap(value, axis):
    return lax.ppermute(value, axis, [(0, 1), (1, 0)])


def mp_sum(value):
    value = value + swap(value, "c")
    return value + swap(value, "yh")


def dot(a, b):
    return jnp.dot(a, b, preferred_element_type=jnp.float32)


def exchange_slots(rows):
    count, width = rows.shape
    rows = rows.reshape(64, count * width // (64 * 128), 128)
    return lax.all_to_all(rows, DP, split_axis=0, concat_axis=0, tiled=True).reshape(count, width)


def split_two(value):
    high = lax.reduce_precision(value, 8, 7)
    return high.astype(jnp.bfloat16), (value - high).astype(jnp.bfloat16)


def body(
    tokens,
    routes,
    expert_gate_affinity,
    expert_gate_weight,
    expert_up_weight,
    expert_down_weight,
    proj,
    student_hidden_input,
    student_norm_weight,
    adapter_down_matrix,
    adapter_up_matrix,
):
    experts = 64
    mp_count = 4
    tok_rows, part_width = tokens.shape
    topk_count = routes.shape[1]
    assigned = tok_rows * topk_count
    capacity = 5
    slot_count = experts * capacity
    rank = adapter_up_matrix.shape[0]
    xi, yh, core = lax.axis_index("x"), lax.axis_index("yh"), lax.axis_index("c")
    mi = yh * 2 + core

    flat_routes = routes.reshape(assigned)
    onehot_e = (flat_routes[:, None] == jnp.arange(experts, dtype=jnp.int32)[None, :]).astype(
        jnp.int32
    )
    position = jnp.sum((jnp.cumsum(onehot_e, axis=0) - onehot_e) * onehot_e, axis=1)
    slot_index = flat_routes * capacity + position
    slot_hit = (jnp.arange(slot_count, dtype=jnp.int32)[:, None] == slot_index[None, :]).astype(
        jnp.bfloat16
    )
    token_hit = (
        jnp.arange(assigned, dtype=jnp.int32)[:, None] // topk_count
        == jnp.arange(tok_rows, dtype=jnp.int32)[None, :]
    ).astype(jnp.bfloat16)
    placing = dot(slot_hit, token_hit).astype(jnp.bfloat16)
    outgoing = dot(placing, tokens).astype(jnp.bfloat16)
    arrived = exchange_slots(outgoing)

    student = student_hidden_input.astype(jnp.float32)
    gain = student_norm_weight.astype(jnp.float32)
    student_width = student.shape[1] * mp_count
    square_sum = jnp.sum(student * student, axis=-1, keepdims=True)
    low_part = dot((student * gain).astype(jnp.bfloat16), adapter_down_matrix)
    proj_low = lax.dot_general(
        proj, adapter_up_matrix, (((1,), (1,)), ((), ())), preferred_element_type=jnp.float32
    )
    stats = jnp.concatenate(
        [low_part, jnp.broadcast_to(square_sum, (tok_rows, rank))], axis=1
    )
    shared = mp_sum(
        jnp.concatenate([stats, jnp.concatenate([proj_low, jnp.zeros_like(proj_low)], axis=1)])
    )
    stats, proj_low = shared[:tok_rows], shared[tok_rows:, :rank]
    inverse = lax.rsqrt(stats[:, rank : rank + 1] / student_width + 1e-06)
    lowrank = (stats[:, :rank] * inverse).astype(jnp.bfloat16)
    normed = (student * inverse * gain).astype(jnp.bfloat16)
    student_out = student + adapter_scale_factor * dot(lowrank, adapter_up_matrix)
    student_back = mp_sum(
        lax.dot_general(
            student_out,
            adapter_up_matrix.astype(jnp.float32),
            (((1,), (1,)), ((), ())),
            precision=lax.Precision.HIGHEST,
        )
    )

    proj_block = lax.all_gather(
        lax.ppermute(jnp.concatenate([proj, *split_two(proj_low)], axis=1), ALL, proj_perm()),
        ("yl", "z"),
        axis=0,
        tiled=True,
    )
    arrived, lowrank = lax.optimization_barrier((arrived, lowrank))

    arrived_y = swap(arrived, "yh")
    arrived_c = swap(arrived, "c")
    arrived_yc = swap(arrived_y, "c")
    parts = (
        (arrived, mi),
        (arrived_c, yh * 2 + 1 - core),
        (arrived_y, (1 - yh) * 2 + core),
        (arrived_yc, (1 - yh) * 2 + 1 - core),
    )
    gate_proj = up_proj = 0.0
    for rows, place in parts:
        gate_proj = gate_proj + dot(
            rows, lax.dynamic_slice_in_dim(expert_gate_weight[0], place * part_width, part_width, 0)
        )
        up_proj = up_proj + dot(
            rows, lax.dynamic_slice_in_dim(expert_up_weight[0], place * part_width, part_width, 0)
        )
    hidden = (jax.nn.silu(gate_proj) * up_proj).astype(jnp.bfloat16)

    def out_part(place):
        return dot(
            hidden, lax.dynamic_slice_in_dim(expert_down_weight[0], place * part_width, part_width, 1)
        )

    far = swap(out_part((1 - yh) * 2 + 1 - core).astype(jnp.bfloat16), "c")
    near = swap(out_part(yh * 2 + 1 - core).astype(jnp.bfloat16), "c")
    far = out_part((1 - yh) * 2 + core).astype(jnp.bfloat16).astype(jnp.float32) + far.astype(
        jnp.float32
    )
    far = swap(far.astype(jnp.bfloat16), "yh")
    expert_out = (
        out_part(mi).astype(jnp.bfloat16).astype(jnp.float32)
        + near.astype(jnp.float32)
        + far.astype(jnp.float32)
    ).astype(jnp.bfloat16)
    returned, student_back = lax.optimization_barrier((exchange_slots(expert_out), student_back))

    weights = (
        route_scale * expert_gate_affinity / jnp.sum(expert_gate_affinity, axis=-1, keepdims=True)
    )
    combine = jnp.dot(
        slot_hit.astype(jnp.float32) * weights.reshape(assigned)[None, :],
        token_hit.astype(jnp.float32),
        precision=lax.Precision.HIGHEST,
    )
    teacher = lax.dot_general(
        combine,
        returned.astype(jnp.float32),
        (((0,), (0,)), ((), ())),
        precision=lax.Precision.HIGHEST,
    ).astype(jnp.bfloat16)

    teacher_rows = lax.all_gather(teacher, "x", axis=0, tiled=True)
    product = dot(teacher_rows, proj_block)
    columns = adapter_up_matrix.shape[1]
    low = product[:, columns : columns + rank] + product[:, columns + rank :]
    product = jnp.concatenate(
        [product[:, :columns].astype(jnp.bfloat16), *split_two(low)], axis=1
    )
    total = 0.0
    for step in range(mp_count):
        block = lax.rem(xi + mi + step, 4)
        piece = lax.dynamic_slice_in_dim(product, block * tok_rows, tok_rows, 0)
        total = total + lax.ppermute(piece, ALL, home_perm(step)).astype(jnp.float32)
    target = total[:, :columns]

    output_difference = student_out - target
    tokens_all = tok_rows * experts
    scale = 1.0 / math.sqrt(tokens_all)
    scaled = (output_difference * scale).astype(jnp.bfloat16)
    loss_here = jnp.sum(output_difference * output_difference)
    teacher_back = total[:, columns : columns + rank] + total[:, columns + rank :]
    back_low = (adapter_scale_factor * scale * (student_back - teacher_back)).astype(jnp.bfloat16)
    over_tokens = (((0,), (0,)), ((), ()))
    up_part = adapter_scale_factor * lax.dot_general(
        lowrank, scaled, over_tokens, preferred_element_type=jnp.float32
    )
    down_part = lax.dot_general(back_low, normed, over_tokens, preferred_element_type=jnp.float32)

    lanes = 128
    blocks = columns // lanes
    first = lax.reduce_precision(loss_here, 8, 7)
    second = lax.reduce_precision(loss_here - first, 8, 7)
    third = loss_here - first - second
    lane = jnp.arange(lanes)
    loss_row = jnp.where(
        lane == 0, first, jnp.where(lane == 1, second, jnp.where(lane == 2, third, 0.0))
    )
    bundle = jnp.concatenate(
        [
            up_part.reshape(rank, blocks, lanes),
            down_part.reshape(rank, blocks, lanes),
            jnp.broadcast_to(loss_row, (rank, 1, lanes)),
        ],
        axis=1,
    ).astype(jnp.bfloat16)
    bundle = lax.all_to_all(bundle, DP, split_axis=0, concat_axis=0, tiled=True)
    summed = jnp.sum(bundle.astype(jnp.float32), axis=0)
    loss_row = summed[2 * blocks :]
    cross = [(i, 3 - i) for i in range(4)]
    loss_row = (loss_row + swap(loss_row, "c")) + (
        swap(loss_row, "yh") + lax.ppermute(loss_row, MP, cross)
    )
    loss = jnp.sum(loss_row) / (tokens_all * student_width)
    grads = jnp.broadcast_to(
        summed[: 2 * blocks].astype(jnp.bfloat16), (rank, 2 * blocks, lanes)
    )
    grads = lax.all_to_all(grads, DP, split_axis=0, concat_axis=0, tiled=True).astype(jnp.float32)
    up_matrix_gradient = grads[:, :blocks].reshape(rank, columns)
    grad_a = grads[:, blocks:].reshape(rank, columns).T
    return (target, grad_a, up_matrix_gradient, loss)


def solution(mesh):
    fine = Mesh(mesh.devices.reshape(SIZES), ALL)
    placed = (
        P(DP, MP),
        P(DP, None),
        P(DP, None),
        P(DP, None, MP),
        P(DP, None, MP),
        P(DP, MP, None),
        P(DP, MP),
        P(DP, MP),
        P(MP),
        P(MP, None),
        P(None, MP),
    )
    return jax.shard_map(
        body,
        mesh=fine,
        in_specs=placed,
        out_specs=(P(DP, MP), P(MP, None), P(None, MP), P()),
        check_vma=False,
    )
```

```python
import math

import jax
import jax.numpy as jnp
from jax import lax
from jax.experimental import pallas as pl
from jax.experimental.pallas import tpu as pltpu
from jax.sharding import Mesh, PartitionSpec as P

route_scale = 2.5
adapter_scale_factor = 0.25
DP = ("yl", "z", "x")
MP = ("yh", "c")
ALL = DP + MP
SIZES = (2, 8, 4, 2, 2)


def index_of(yl, z, x, yh, c):
    return (((yl * 8 + z) * 4 + x) * 2 + yh) * 2 + c


def coords():
    for yl in range(2):
        for z in range(8):
            for x in range(4):
                for yh in range(2):
                    for c in range(2):
                        yield yl, z, x, yh, c


def proj_perm(step):
    pairs = []
    for yl, z, x, yh, c in coords():
        pairs.append(
            (index_of(yl, z, x, yh, c), index_of(x // 2, z, yh * 2 + c, yl, step ^ (x % 2)))
        )
    return pairs


def home_perm(step):
    pairs = []
    for yl, z, x, yh, c in coords():
        m = yh * 2 + c
        pairs.append(
            (index_of(yl, z, x, yh, c), index_of(yl, z, x ^ m ^ step, x // 2, x % 2))
        )
    return pairs


def swap(value, axis):
    return lax.ppermute(value, axis, [(0, 1), (1, 0)])


def mp_sum(value):
    value = value + swap(value, "c")
    return value + swap(value, "yh")


def dot(a, b):
    return jnp.dot(a, b, preferred_element_type=jnp.float32)


def exchange_slots(rows):
    count, width = rows.shape
    rows = rows.reshape(64, count * width // (64 * 128), 128)
    return lax.all_to_all(rows, DP, split_axis=0, concat_axis=0, tiled=True).reshape(count, width)


def split_two(value):
    high = lax.reduce_precision(value, 8, 7)
    return high.astype(jnp.bfloat16), (value - high).astype(jnp.bfloat16)


def product_kernel(order_ref, own_ref, other_ref, block_ref, *refs):
    outs, total = refs[:4], refs[4]
    width = own_ref.shape[1]
    rows = own_ref.shape[0] // 4
    wide = block_ref.shape[1] - 128
    core = order_ref[4]
    near = block_ref[pl.ds(pl.multiple_of(core * width, 128), width), :]
    far = block_ref[pl.ds(pl.multiple_of((1 - core) * width, 128), width), :]
    total[...] = dot(own_ref[...], near) + dot(other_ref[...], far)
    for step in range(4):
        here = pl.ds(pl.multiple_of(order_ref[step] * rows, 128), rows)
        outs[step][:, :wide] = total[here, :wide].astype(jnp.bfloat16)
        low = total[here, wide:]
        low = low + pltpu.roll(low, 64, 1)
        lane = lax.broadcasted_iota(jnp.int32, low.shape, 1)
        rest = low - low.astype(jnp.bfloat16).astype(jnp.float32)
        outs[step][:, wide:] = jnp.where(lane < 64, low, rest).astype(jnp.bfloat16)


def product_pieces(order, own, other, block):
    rows, wide = own.shape[0], block.shape[1]
    vmem = pl.BlockSpec(memory_space=pltpu.VMEM)
    return pl.pallas_call(
        product_kernel,
        out_shape=[jax.ShapeDtypeStruct((rows // 4, wide), jnp.bfloat16)] * 4,
        in_specs=[pl.BlockSpec(memory_space=pltpu.SMEM), vmem, vmem, vmem],
        out_specs=[vmem] * 4,
        scratch_shapes=[pltpu.VMEM((rows, wide), jnp.float32)],
        compiler_params=pltpu.CompilerParams(vmem_limit_bytes=40 * 1024 * 1024),
        cost_estimate=pl.CostEstimate(
            flops=4 * rows * own.shape[1] * wide, bytes_accessed=8_000_000, transcendentals=0
        ),
    )(order, own, other, block)


def body(
    tokens,
    routes,
    expert_gate_affinity,
    expert_gate_weight,
    expert_up_weight,
    expert_down_weight,
    proj,
    student_hidden_input,
    student_norm_weight,
    adapter_down_matrix,
    adapter_up_matrix,
):
    experts = 64
    mp_count = 4
    tok_rows, part_width = tokens.shape
    topk_count = routes.shape[1]
    assigned = tok_rows * topk_count
    capacity = 5
    slot_count = experts * capacity
    rank = adapter_up_matrix.shape[0]
    xi, yh, core = lax.axis_index("x"), lax.axis_index("yh"), lax.axis_index("c")
    yl = lax.axis_index("yl")
    mi = yh * 2 + core

    flat_routes = routes.reshape(assigned)
    onehot_e = (flat_routes[:, None] == jnp.arange(experts, dtype=jnp.int32)[None, :]).astype(
        jnp.int32
    )
    position = jnp.sum((jnp.cumsum(onehot_e, axis=0) - onehot_e) * onehot_e, axis=1)
    slot_index = flat_routes * capacity + position
    slot_hit = (jnp.arange(slot_count, dtype=jnp.int32)[:, None] == slot_index[None, :]).astype(
        jnp.bfloat16
    )
    token_hit = (
        jnp.arange(assigned, dtype=jnp.int32)[:, None] // topk_count
        == jnp.arange(tok_rows, dtype=jnp.int32)[None, :]
    ).astype(jnp.bfloat16)
    placing = dot(slot_hit, token_hit).astype(jnp.bfloat16)
    outgoing = dot(placing, tokens).astype(jnp.bfloat16)

    student = student_hidden_input.astype(jnp.float32)
    gain = student_norm_weight.astype(jnp.float32)
    student_width = student.shape[1] * mp_count
    square_sum = jnp.sum(student * student, axis=-1, keepdims=True)
    low_part = dot((student * gain).astype(jnp.bfloat16), adapter_down_matrix)
    proj_low = lax.dot_general(
        proj, adapter_up_matrix, (((1,), (1,)), ((), ())), preferred_element_type=jnp.float32
    )
    stats = jnp.concatenate(
        [low_part, jnp.broadcast_to(square_sum, (tok_rows, rank))], axis=1
    )
    shared = jnp.concatenate(
        [stats, jnp.concatenate([proj_low, jnp.zeros_like(proj_low)], axis=1)]
    )
    outgoing, shared = lax.optimization_barrier((outgoing, shared + swap(shared, "c")))
    arrived = exchange_slots(outgoing)
    shared = shared + swap(shared, "yh")
    stats, proj_low = shared[:tok_rows], shared[tok_rows:, :rank]

    half = proj.shape[1] // 2
    extra = split_two(proj_low)
    halves = []
    for step in range(2):
        mine = lax.dynamic_slice_in_dim(proj, (step ^ (xi & 1)) * half, half, 1)
        halves.append(
            lax.ppermute(jnp.concatenate([mine, *extra], axis=1), ALL, proj_perm(step))
        )
    halves = jnp.where(
        core == 0, jnp.concatenate(halves), jnp.concatenate([halves[1], halves[0]])
    )
    others = swap(halves, "yl")
    halves = jnp.where(
        yl == 0, jnp.concatenate([halves, others]), jnp.concatenate([others, halves])
    )
    proj_block = lax.all_gather(halves, "z", axis=0, tiled=True)

    inverse = lax.rsqrt(stats[:, rank : rank + 1] / student_width + 1e-06)
    lowrank = (stats[:, :rank] * inverse).astype(jnp.bfloat16)
    normed = (student * inverse * gain).astype(jnp.bfloat16)
    student_out = student + adapter_scale_factor * dot(lowrank, adapter_up_matrix)
    student_back = mp_sum(
        lax.dot_general(
            student_out,
            adapter_up_matrix.astype(jnp.float32),
            (((1,), (1,)), ((), ())),
            precision=lax.Precision.HIGHEST,
        )
    )

    arrived_y = swap(arrived, "yh")
    arrived_c = swap(arrived, "c")
    arrived_yc = swap(arrived_y, "c")
    parts = (
        (arrived, mi),
        (arrived_c, yh * 2 + 1 - core),
        (arrived_y, (1 - yh) * 2 + core),
        (arrived_yc, (1 - yh) * 2 + 1 - core),
    )
    gate_proj = up_proj = 0.0
    for rows, place in parts:
        gate_proj = gate_proj + dot(
            rows, lax.dynamic_slice_in_dim(expert_gate_weight[0], place * part_width, part_width, 0)
        )
        up_proj = up_proj + dot(
            rows, lax.dynamic_slice_in_dim(expert_up_weight[0], place * part_width, part_width, 0)
        )
    hidden = (jax.nn.silu(gate_proj) * up_proj).astype(jnp.bfloat16)

    def out_part(place):
        return dot(
            hidden, lax.dynamic_slice_in_dim(expert_down_weight[0], place * part_width, part_width, 1)
        )

    far = swap(out_part((1 - yh) * 2 + 1 - core).astype(jnp.bfloat16), "c")
    near = swap(out_part(yh * 2 + 1 - core).astype(jnp.bfloat16), "c")
    far = out_part((1 - yh) * 2 + core).astype(jnp.bfloat16).astype(jnp.float32) + far.astype(
        jnp.float32
    )
    far = swap(far.astype(jnp.bfloat16), "yh")
    expert_out = (
        out_part(mi).astype(jnp.bfloat16).astype(jnp.float32)
        + near.astype(jnp.float32)
        + far.astype(jnp.float32)
    ).astype(jnp.bfloat16)
    returned, student_back = lax.optimization_barrier((exchange_slots(expert_out), student_back))

    weights = (
        route_scale * expert_gate_affinity / jnp.sum(expert_gate_affinity, axis=-1, keepdims=True)
    )
    combine = jnp.dot(
        slot_hit.astype(jnp.float32) * weights.reshape(assigned)[None, :],
        token_hit.astype(jnp.float32),
        precision=lax.Precision.HIGHEST,
    )
    teacher = lax.dot_general(
        combine,
        returned.astype(jnp.float32),
        (((0,), (0,)), ((), ())),
        precision=lax.Precision.HIGHEST,
    ).astype(jnp.bfloat16)

    teacher_rows = lax.all_gather(teacher, "x", axis=0, tiled=True)
    order = jnp.stack([xi ^ mi ^ step for step in range(mp_count)] + [core])
    pieces = product_pieces(order, teacher_rows, swap(teacher_rows, "c"), proj_block)
    pieces = [
        lax.ppermute(piece, ALL, home_perm(step)).astype(jnp.float32)
        for step, piece in enumerate(pieces)
    ]
    even, odd = pieces[0] + pieces[2], pieces[1] + pieces[3]
    first_even = (xi ^ mi) & 1 == 0
    left, right = even[:, :half], odd[:, :half]
    target = jnp.where(
        first_even,
        jnp.concatenate([left, right], axis=1),
        jnp.concatenate([right, left], axis=1),
    )
    teacher_back = even[:, half : half + rank] + even[:, half + rank :]

    output_difference = student_out - target
    tokens_all = tok_rows * experts
    scale = 1.0 / math.sqrt(tokens_all)
    scaled = (output_difference * scale).astype(jnp.bfloat16)
    loss_here = jnp.sum(output_difference * output_difference)
    back_low = (adapter_scale_factor * scale * (student_back - teacher_back)).astype(jnp.bfloat16)
    over_tokens = (((0,), (0,)), ((), ()))
    up_part = adapter_scale_factor * lax.dot_general(
        lowrank, scaled, over_tokens, preferred_element_type=jnp.float32
    )
    down_part = lax.dot_general(back_low, normed, over_tokens, preferred_element_type=jnp.float32)

    lanes = 128
    columns = up_part.shape[1]
    tiles = rank // 8 * (columns // lanes)
    first = lax.reduce_precision(loss_here, 8, 7)
    second = lax.reduce_precision(loss_here - first, 8, 7)
    third = loss_here - first - second
    lane = jnp.arange(lanes)
    loss_row = jnp.where(
        lane == 0, first, jnp.where(lane == 1, second, jnp.where(lane == 2, third, 0.0))
    )

    def to_tiles(value):
        value = value.astype(jnp.bfloat16).reshape(rank // 8, 8, columns // lanes, lanes)
        return value.transpose(0, 2, 1, 3).reshape(tiles, 8, lanes)

    def from_tiles(value):
        value = value.reshape(rank // 8, columns // lanes, 8, lanes).transpose(0, 2, 1, 3)
        return value.reshape(rank, columns).astype(jnp.float32)

    bundle = jnp.concatenate([to_tiles(up_part), to_tiles(down_part)])
    bundle = jnp.concatenate(
        [
            bundle[: 2 * experts].reshape(experts, 16, lanes),
            bundle[2 * experts :].reshape(experts, 4, lanes),
            jnp.broadcast_to(loss_row.astype(jnp.bfloat16), (experts, 4, lanes)),
        ],
        axis=1,
    )
    bundle = lax.all_to_all(bundle, DP, split_axis=0, concat_axis=0, tiled=True)
    summed = jnp.sum(bundle.astype(jnp.float32), axis=0)
    grads = jnp.broadcast_to(summed.astype(jnp.bfloat16), (experts, 24, lanes))
    grads = lax.all_to_all(grads, DP, split_axis=0, concat_axis=0, tiled=True)
    loss_row = summed[20:21]
    cross = [(i, 3 - i) for i in range(4)]
    loss_row = (loss_row + swap(loss_row, "c")) + (
        swap(loss_row, "yh") + lax.ppermute(loss_row, MP, cross)
    )
    loss = jnp.sum(loss_row) / (tokens_all * student_width)
    grads = jnp.concatenate(
        [
            grads[:, :16].reshape(2 * experts, 8, lanes),
            grads[:, 16:20].reshape(experts // 2, 8, lanes),
        ]
    )
    up_matrix_gradient = from_tiles(grads[:tiles])
    grad_a = from_tiles(grads[tiles:]).T
    return (target, grad_a, up_matrix_gradient, loss)


def solution(mesh):
    fine = Mesh(mesh.devices.reshape(SIZES), ALL)
    placed = (
        P(DP, MP),
        P(DP, None),
        P(DP, None),
        P(DP, None, MP),
        P(DP, None, MP),
        P(DP, MP, None),
        P(DP, MP),
        P(DP, MP),
        P(MP),
        P(MP, None),
        P(None, MP),
    )
    return jax.shard_map(
        body,
        mesh=fine,
        in_specs=placed,
        out_specs=(P(DP, MP), P(MP, None), P(None, MP), P()),
        check_vma=False,
    )
```

```python
import itertools
import math

import jax
import jax.numpy as jnp
from jax import lax
from jax.experimental import pallas as pl
from jax.experimental.pallas import tpu as pltpu
from jax.sharding import Mesh, PartitionSpec as P

route_scale = 2.5
adapter_scale_factor = 0.25
DP = ("yl", "z", "xh", "xl")
MP = ("yh", "c")
ALL = DP + MP
SIZES = (2, 8, 2, 2, 2, 2)


def permutation(target):
    places = list(itertools.product(*(range(size) for size in SIZES)))
    return [(place, places.index(target(*here))) for place, here in enumerate(places)]


def proj_target(yl, z, xh, xl, yh, c):
    return (xh, z, xl, yh, yl, c)


def home_target(step):
    return lambda yl, z, xh, xl, yh, c: (yl, z, xh, yh ^ step, xl, c)


def swap(value, axis):
    return lax.ppermute(value, axis, [(0, 1), (1, 0)])


def mp_sum(value):
    value = value + swap(value, "c")
    return value + swap(value, "yh")


def dot(a, b):
    return jnp.dot(a, b, preferred_element_type=jnp.float32)


def pair_rows(value, axis, index):
    other = swap(value, axis)
    return jnp.where(
        index == 0, jnp.concatenate([value, other]), jnp.concatenate([other, value])
    )


def exchange_slots(rows):
    count, width = rows.shape
    rows = rows.reshape(64, count * width // (64 * 128), 128)
    return lax.all_to_all(rows, DP, split_axis=0, concat_axis=0, tiled=True).reshape(count, width)


def product_kernel(order_ref, own_ref, own_far_ref, pair_ref, pair_far_ref, block_ref, *refs):
    outs, near_rows, far_rows, total = refs[:2], refs[2], refs[3], refs[4]
    rows, width = own_ref.shape

    @pl.when(pl.program_id(0) == 0)
    def _():
        near_rows[:rows] = own_ref[...]
        near_rows[rows:] = pair_ref[...]
        far_rows[:rows] = own_far_ref[...]
        far_rows[rows:] = pair_far_ref[...]

    core = order_ref[2]
    near = block_ref[pl.ds(pl.multiple_of(core * width, 128), width), :]
    far = block_ref[pl.ds(pl.multiple_of((1 - core) * width, 128), width), :]
    total[...] = dot(near_rows[...], near) + dot(far_rows[...], far)
    for step in range(2):
        here = pl.ds(pl.multiple_of(order_ref[step] * rows, 128), rows)
        outs[step][...] = total[here, :].astype(jnp.bfloat16)


def product_pieces(order, own, own_far, pair, pair_far, block):
    rows, width = own.shape
    depth, wide = block.shape
    cut = 256
    whole = pl.BlockSpec((rows, width), lambda i: (0, 0))
    return pl.pallas_call(
        product_kernel,
        grid=(wide // cut,),
        out_shape=[jax.ShapeDtypeStruct((rows, wide), jnp.bfloat16)] * 2,
        in_specs=[pl.BlockSpec(memory_space=pltpu.SMEM)]
        + [whole] * 4
        + [pl.BlockSpec((depth, cut), lambda i: (0, i))],
        out_specs=[pl.BlockSpec((rows, cut), lambda i: (0, i))] * 2,
        scratch_shapes=[
            pltpu.VMEM((2 * rows, width), jnp.bfloat16),
            pltpu.VMEM((2 * rows, width), jnp.bfloat16),
            pltpu.VMEM((2 * rows, cut), jnp.float32),
        ],
        compiler_params=pltpu.CompilerParams(vmem_limit_bytes=24 * 1024 * 1024),
        cost_estimate=pl.CostEstimate(
            flops=4 * rows * depth * wide, bytes_accessed=6_000_000, transcendentals=0
        ),
    )(order, own, own_far, pair, pair_far, block)


def body(
    tokens,
    routes,
    expert_gate_affinity,
    expert_gate_weight,
    expert_up_weight,
    expert_down_weight,
    proj,
    student_hidden_input,
    student_norm_weight,
    adapter_down_matrix,
    adapter_up_matrix,
):
    experts = 64
    mp_count = 4
    tok_rows, part_width = tokens.shape
    topk_count = routes.shape[1]
    assigned = tok_rows * topk_count
    capacity = 5
    slot_count = experts * capacity
    rank = adapter_up_matrix.shape[0]
    yl, xh, xl, yh, core = (lax.axis_index(name) for name in ("yl", "xh", "xl", "yh", "c"))
    mi = yh * 2 + core

    proj_rows = lax.ppermute(proj, ALL, permutation(proj_target))

    flat_routes = routes.reshape(assigned)
    onehot_e = (flat_routes[:, None] == jnp.arange(experts, dtype=jnp.int32)[None, :]).astype(
        jnp.int32
    )
    position = jnp.sum((jnp.cumsum(onehot_e, axis=0) - onehot_e) * onehot_e, axis=1)
    slot_index = flat_routes * capacity + position
    slot_hit = (jnp.arange(slot_count, dtype=jnp.int32)[:, None] == slot_index[None, :]).astype(
        jnp.bfloat16
    )
    token_hit = (
        jnp.arange(assigned, dtype=jnp.int32)[:, None] // topk_count
        == jnp.arange(tok_rows, dtype=jnp.int32)[None, :]
    ).astype(jnp.bfloat16)
    placing = dot(slot_hit, token_hit).astype(jnp.bfloat16)
    outgoing = dot(placing, tokens).astype(jnp.bfloat16)

    outgoing, proj_rows = lax.optimization_barrier((outgoing, proj_rows))
    arrived = exchange_slots(outgoing)
    proj_rows = pair_rows(proj_rows, "xh", xh)
    proj_rows = pair_rows(proj_rows, "yl", yl)
    arrived, proj_rows = lax.optimization_barrier((arrived, proj_rows))
    proj_block = lax.all_gather(proj_rows, "z", axis=0, tiled=True)

    arrived_y = swap(arrived, "yh")
    arrived_c = swap(arrived, "c")
    arrived_yc = swap(arrived_y, "c")
    parts = (
        (arrived, mi),
        (arrived_c, yh * 2 + 1 - core),
        (arrived_y, (1 - yh) * 2 + core),
        (arrived_yc, (1 - yh) * 2 + 1 - core),
    )
    gate_proj = up_proj = 0.0
    for rows, place in parts:
        gate_proj = gate_proj + dot(
            rows, lax.dynamic_slice_in_dim(expert_gate_weight[0], place * part_width, part_width, 0)
        )
        up_proj = up_proj + dot(
            rows, lax.dynamic_slice_in_dim(expert_up_weight[0], place * part_width, part_width, 0)
        )
    hidden = (jax.nn.silu(gate_proj) * up_proj).astype(jnp.bfloat16)

    def out_part(place):
        return dot(
            hidden, lax.dynamic_slice_in_dim(expert_down_weight[0], place * part_width, part_width, 1)
        )

    far = swap(out_part((1 - yh) * 2 + 1 - core).astype(jnp.bfloat16), "c")
    near = swap(out_part(yh * 2 + 1 - core).astype(jnp.bfloat16), "c")
    far = out_part((1 - yh) * 2 + core).astype(jnp.bfloat16).astype(jnp.float32) + far.astype(
        jnp.float32
    )
    far = swap(far.astype(jnp.bfloat16), "yh")
    expert_out = (
        out_part(mi).astype(jnp.bfloat16).astype(jnp.float32)
        + near.astype(jnp.float32)
        + far.astype(jnp.float32)
    ).astype(jnp.bfloat16)
    returned = exchange_slots(expert_out)

    expert_out, student_hidden_input = lax.optimization_barrier((expert_out, student_hidden_input))
    student = student_hidden_input.astype(jnp.float32)
    gain = student_norm_weight.astype(jnp.float32)
    student_width = student.shape[1] * mp_count
    square_sum = jnp.sum(student * student, axis=-1, keepdims=True)
    low_part = dot((student * gain).astype(jnp.bfloat16), adapter_down_matrix)
    stats = mp_sum(
        jnp.concatenate([low_part, jnp.broadcast_to(square_sum, (tok_rows, rank))], axis=1)
    )
    inverse = lax.rsqrt(stats[:, rank : rank + 1] / student_width + 1e-06)
    lowrank = (stats[:, :rank] * inverse).astype(jnp.bfloat16)
    normed = (student * inverse * gain).astype(jnp.bfloat16)
    student_out = student + adapter_scale_factor * dot(lowrank, adapter_up_matrix)
    returned, lowrank, normed, student_out = lax.optimization_barrier(
        (returned, lowrank, normed, student_out)
    )


    weights = (
        route_scale * expert_gate_affinity / jnp.sum(expert_gate_affinity, axis=-1, keepdims=True)
    )
    combine = jnp.dot(
        slot_hit.astype(jnp.float32) * weights.reshape(assigned)[None, :],
        token_hit.astype(jnp.float32),
        precision=lax.Precision.HIGHEST,
    )
    teacher = lax.dot_general(
        combine,
        returned.astype(jnp.float32),
        (((0,), (0,)), ((), ())),
        precision=lax.Precision.HIGHEST,
    ).astype(jnp.bfloat16)

    teacher_far = swap(teacher, "c")
    pair = swap(teacher, "xl")
    order = jnp.stack([yh ^ xl, yh ^ xl ^ 1, core])
    pieces = product_pieces(order, teacher, teacher_far, pair, swap(pair, "c"), proj_block)
    pieces = [
        lax.ppermute(piece, ALL, permutation(home_target(step))).astype(jnp.float32)
        for step, piece in enumerate(pieces)
    ]
    target = pieces[0] + pieces[1]

    output_difference = student_out - target
    tokens_all = tok_rows * experts
    scale = 1.0 / math.sqrt(tokens_all)
    scaled = (output_difference * scale).astype(jnp.bfloat16)
    loss_here = jnp.sum(output_difference * output_difference)
    back_part = lax.dot_general(
        scaled, adapter_up_matrix, (((1,), (1,)), ((), ())), preferred_element_type=jnp.float32
    )
    back_low = (adapter_scale_factor * mp_sum(back_part)).astype(jnp.bfloat16)
    over_tokens = (((0,), (0,)), ((), ()))
    up_part = adapter_scale_factor * lax.dot_general(
        lowrank, scaled, over_tokens, preferred_element_type=jnp.float32
    )
    down_part = lax.dot_general(back_low, normed, over_tokens, preferred_element_type=jnp.float32)

    lanes = 128
    columns = up_part.shape[1]
    tiles = rank // 8 * (columns // lanes)
    first = lax.reduce_precision(loss_here, 8, 7)
    second = lax.reduce_precision(loss_here - first, 8, 7)
    third = loss_here - first - second
    lane = jnp.arange(lanes)
    loss_row = jnp.where(
        lane == 0, first, jnp.where(lane == 1, second, jnp.where(lane == 2, third, 0.0))
    )

    def to_tiles(value):
        value = value.astype(jnp.bfloat16).reshape(rank // 8, 8, columns // lanes, lanes)
        return value.transpose(0, 2, 1, 3).reshape(tiles, 8, lanes)

    def from_tiles(value):
        value = value.reshape(rank // 8, columns // lanes, 8, lanes).transpose(0, 2, 1, 3)
        return value.reshape(rank, columns).astype(jnp.float32)

    bundle = jnp.concatenate([to_tiles(up_part), to_tiles(down_part)])
    bundle = jnp.concatenate(
        [
            bundle[: 2 * experts].reshape(experts, 16, lanes),
            bundle[2 * experts :].reshape(experts, 4, lanes),
            jnp.broadcast_to(loss_row.astype(jnp.bfloat16), (experts, 4, lanes)),
        ],
        axis=1,
    )
    bundle = lax.all_to_all(bundle, DP, split_axis=0, concat_axis=0, tiled=True)
    summed = jnp.sum(bundle.astype(jnp.float32), axis=0)
    grads = jnp.broadcast_to(summed.astype(jnp.bfloat16), (experts, 24, lanes))
    grads = lax.all_to_all(grads, DP, split_axis=0, concat_axis=0, tiled=True)
    loss_row = summed[20:21]
    cross = [(i, 3 - i) for i in range(4)]
    loss_row = (loss_row + swap(loss_row, "c")) + (
        swap(loss_row, "yh") + lax.ppermute(loss_row, MP, cross)
    )
    loss = jnp.sum(loss_row) / (tokens_all * student_width)
    grads = jnp.concatenate(
        [
            grads[:, :16].reshape(2 * experts, 8, lanes),
            grads[:, 16:20].reshape(experts // 2, 8, lanes),
        ]
    )
    up_matrix_gradient = from_tiles(grads[:tiles])
    grad_a = from_tiles(grads[tiles:]).T
    return (target, grad_a, up_matrix_gradient, loss)


def solution(mesh):
    fine = Mesh(mesh.devices.reshape(SIZES), ALL)
    placed = (
        P(DP, MP),
        P(DP, None),
        P(DP, None),
        P(DP, None, MP),
        P(DP, None, MP),
        P(DP, MP, None),
        P(DP, MP),
        P(DP, MP),
        P(MP),
        P(MP, None),
        P(None, MP),
    )
    return jax.shard_map(
        body,
        mesh=fine,
        in_specs=placed,
        out_specs=(P(DP, MP), P(MP, None), P(None, MP), P()),
        check_vma=False,
    )
```

```python
import functools
import itertools
import math

import jax
import jax.numpy as jnp
from jax import lax
from jax.experimental import pallas as pl
from jax.experimental.pallas import tpu as pltpu
from jax.sharding import Mesh, PartitionSpec as P

route_scale = 2.5
adapter_scale_factor = 0.25
DP = ("yl", "z", "xh", "xl")
MP = ("yh", "c")
ALL = DP + MP
SIZES = (2, 8, 2, 2, 2, 2)


def permutation(target):
    places = list(itertools.product(*(range(size) for size in SIZES)))
    return [(place, places.index(target(*here))) for place, here in enumerate(places)]


def proj_target(yl, z, xh, xl, yh, c):
    return (xl, z, xh, yh, yl, c)


def home_target(step):
    return lambda yl, z, xh, xl, yh, c: (yl, z, xh, yh ^ step, xl, c)


def swap(value, axis):
    return lax.ppermute(value, axis, [(0, 1), (1, 0)])


def mp_sum(value):
    value = value + swap(value, "c")
    return value + swap(value, "yh")


def dot(a, b):
    return jnp.dot(a, b, preferred_element_type=jnp.float32)


def pair_rows(value, axis, index):
    other = swap(value, axis)
    return jnp.where(
        index == 0, jnp.concatenate([value, other]), jnp.concatenate([other, value])
    )


def exchange_slots(rows):
    count, width = rows.shape
    rows = rows.reshape(64, count * width // (64 * 128), 128)
    return lax.all_to_all(rows, DP, split_axis=0, concat_axis=0, tiled=True).reshape(count, width)


def product_kernel(order_ref, own_ref, own_far_ref, pair_ref, pair_far_ref, block_ref, *refs):
    outs, near_rows, far_rows, total, held, arrived = refs[:2], *refs[2:]
    rows, width = own_ref.shape
    count, cut = held.shape[0], held.shape[2]
    copies = [
        pltpu.make_async_copy(
            block_ref.at[:, pl.ds(index * cut, cut)], held.at[index], arrived.at[index]
        )
        for index in range(count)
    ]
    for copy in copies:
        copy.start()
    near_rows[:rows] = own_ref[...]
    near_rows[rows:] = pair_ref[...]
    far_rows[:rows] = own_far_ref[...]
    far_rows[rows:] = pair_far_ref[...]
    core = order_ref[2]
    near = pl.ds(pl.multiple_of(core * width, 128), width)
    far = pl.ds(pl.multiple_of((1 - core) * width, 128), width)
    for index, copy in enumerate(copies):
        copy.wait()
        total[...] = dot(near_rows[...], held[index, near, :]) + dot(
            far_rows[...], held[index, far, :]
        )
        for step in range(2):
            here = pl.ds(pl.multiple_of(order_ref[step] * rows, 128), rows)
            outs[step][:, index * cut : (index + 1) * cut] = total[here, :].astype(jnp.bfloat16)


def product_pieces(order, own, own_far, pair, pair_far, block):
    rows, width = own.shape
    depth, wide = block.shape
    cut = 256
    vmem = pl.BlockSpec(memory_space=pltpu.VMEM)
    return pl.pallas_call(
        product_kernel,
        out_shape=[jax.ShapeDtypeStruct((rows, wide), jnp.bfloat16)] * 2,
        in_specs=[pl.BlockSpec(memory_space=pltpu.SMEM)]
        + [vmem] * 4
        + [pl.BlockSpec(memory_space=pltpu.HBM)],
        out_specs=[vmem] * 2,
        scratch_shapes=[
            pltpu.VMEM((2 * rows, width), jnp.bfloat16),
            pltpu.VMEM((2 * rows, width), jnp.bfloat16),
            pltpu.VMEM((2 * rows, cut), jnp.float32),
            pltpu.VMEM((wide // cut, depth, cut), jnp.bfloat16),
            pltpu.SemaphoreType.DMA((wide // cut,)),
        ],
        compiler_params=pltpu.CompilerParams(vmem_limit_bytes=24 * 1024 * 1024),
        cost_estimate=pl.CostEstimate(
            flops=4 * rows * depth * wide, bytes_accessed=6_000_000, transcendentals=0
        ),
    )(order, own, own_far, pair, pair_far, block)


def stats_kernel(student_ref, gain_ref, down_ref, out_ref):
    student = student_ref[...].astype(jnp.float32)
    scaled = (student * gain_ref[...].astype(jnp.float32)).astype(jnp.bfloat16)
    rank = down_ref.shape[0]
    out_ref[:, :rank] = lax.dot_general(
        scaled, down_ref[...], (((1,), (1,)), ((), ())), preferred_element_type=jnp.float32
    )
    total = jnp.sum(student * student, axis=-1, keepdims=True)
    out_ref[:, rank:] = jnp.broadcast_to(total, (student.shape[0], rank))


def student_kernel(width, stats_ref, student_ref, gain_ref, up_ref, low_ref, normed_ref, out_ref):
    rank = up_ref.shape[0]
    inverse = lax.rsqrt(stats_ref[:, rank : rank + 1] / width + 1e-06)
    low = (stats_ref[:, :rank] * inverse).astype(jnp.bfloat16)
    student = student_ref[...].astype(jnp.float32)
    low_ref[...] = low
    normed_ref[...] = (student * inverse * gain_ref[...].astype(jnp.float32)).astype(jnp.bfloat16)
    out_ref[...] = student + adapter_scale_factor * dot(low, up_ref[...])


def local_kernel(kernel, shapes, *args):
    vmem = pl.BlockSpec(memory_space=pltpu.VMEM)
    return pl.pallas_call(
        kernel,
        out_shape=shapes,
        in_specs=[vmem] * len(args),
        out_specs=jax.tree.map(lambda _: vmem, shapes),
        compiler_params=pltpu.CompilerParams(vmem_limit_bytes=16 * 1024 * 1024),
        cost_estimate=pl.CostEstimate(flops=100, bytes_accessed=100, transcendentals=0),
    )(*args)


def body(
    tokens,
    routes,
    expert_gate_affinity,
    expert_gate_weight,
    expert_up_weight,
    expert_down_weight,
    proj,
    student_hidden_input,
    student_norm_weight,
    adapter_down_matrix,
    adapter_up_matrix,
):
    experts = 64
    mp_count = 4
    tok_rows, part_width = tokens.shape
    topk_count = routes.shape[1]
    assigned = tok_rows * topk_count
    capacity = 5
    slot_count = experts * capacity
    rank = adapter_up_matrix.shape[0]
    yl, xh, xl, yh, core = (lax.axis_index(name) for name in ("yl", "xh", "xl", "yh", "c"))
    mi = yh * 2 + core

    flat_routes = routes.reshape(assigned)
    onehot_e = (flat_routes[:, None] == jnp.arange(experts, dtype=jnp.int32)[None, :]).astype(
        jnp.int32
    )
    position = jnp.sum((jnp.cumsum(onehot_e, axis=0) - onehot_e) * onehot_e, axis=1)
    slot_index = flat_routes * capacity + position
    slot_hit = (jnp.arange(slot_count, dtype=jnp.int32)[:, None] == slot_index[None, :]).astype(
        jnp.bfloat16
    )
    token_hit = (
        jnp.arange(assigned, dtype=jnp.int32)[:, None] // topk_count
        == jnp.arange(tok_rows, dtype=jnp.int32)[None, :]
    ).astype(jnp.bfloat16)
    placing = dot(slot_hit, token_hit).astype(jnp.bfloat16)
    outgoing = dot(placing, tokens).astype(jnp.bfloat16)

    outgoing, proj = lax.optimization_barrier((outgoing, proj))
    arrived = exchange_slots(outgoing)

    proj_rows = lax.ppermute(proj, ALL, permutation(proj_target))
    proj_rows = pair_rows(proj_rows, "yl", yl)
    arrived, proj_rows = lax.optimization_barrier((arrived, proj_rows))

    arrived_y = swap(arrived, "yh")
    arrived_c = swap(arrived, "c")
    proj_rows = pair_rows(proj_rows, "xh", xh)

    gain = student_norm_weight.reshape(1, -1)
    stats = local_kernel(
        stats_kernel,
        jax.ShapeDtypeStruct((tok_rows, 2 * rank), jnp.float32),
        student_hidden_input,
        gain,
        adapter_down_matrix.T,
    )
    stats = stats + swap(stats, "c")
    arrived_y, proj_rows, stats = lax.optimization_barrier((arrived_y, proj_rows, stats))
    proj_block = lax.all_gather(proj_rows, "z", axis=0, tiled=True)
    arrived_yc = swap(arrived_y, "c")
    parts = (
        (arrived, mi),
        (arrived_c, yh * 2 + 1 - core),
        (arrived_y, (1 - yh) * 2 + core),
        (arrived_yc, (1 - yh) * 2 + 1 - core),
    )
    gate_proj = up_proj = 0.0
    for rows, place in parts:
        gate_proj = gate_proj + dot(
            rows, lax.dynamic_slice_in_dim(expert_gate_weight[0], place * part_width, part_width, 0)
        )
        up_proj = up_proj + dot(
            rows, lax.dynamic_slice_in_dim(expert_up_weight[0], place * part_width, part_width, 0)
        )
    hidden = (jax.nn.silu(gate_proj) * up_proj).astype(jnp.bfloat16)

    def out_part(place):
        return dot(
            hidden, lax.dynamic_slice_in_dim(expert_down_weight[0], place * part_width, part_width, 1)
        )

    far = swap(out_part((1 - yh) * 2 + 1 - core).astype(jnp.bfloat16), "c")
    near = swap(out_part(yh * 2 + 1 - core).astype(jnp.bfloat16), "c")
    far = out_part((1 - yh) * 2 + core).astype(jnp.bfloat16).astype(jnp.float32) + far.astype(
        jnp.float32
    )
    far = swap(far.astype(jnp.bfloat16), "yh")
    expert_out = (
        out_part(mi).astype(jnp.bfloat16).astype(jnp.float32)
        + near.astype(jnp.float32)
        + far.astype(jnp.float32)
    ).astype(jnp.bfloat16)
    returned = exchange_slots(expert_out)

    stats = stats + swap(stats, "yh")
    student_width = student_hidden_input.shape[1] * mp_count
    lowrank, normed, student_out = local_kernel(
        functools.partial(student_kernel, student_width),
        [
            jax.ShapeDtypeStruct((tok_rows, rank), jnp.bfloat16),
            jax.ShapeDtypeStruct(student_hidden_input.shape, jnp.bfloat16),
            jax.ShapeDtypeStruct(student_hidden_input.shape, jnp.float32),
        ],
        stats,
        student_hidden_input,
        gain,
        adapter_up_matrix,
    )
    returned, lowrank, normed, student_out = lax.optimization_barrier(
        (returned, lowrank, normed, student_out)
    )

    weights = (
        route_scale * expert_gate_affinity / jnp.sum(expert_gate_affinity, axis=-1, keepdims=True)
    )
    combine = jnp.dot(
        slot_hit.astype(jnp.float32) * weights.reshape(assigned)[None, :],
        token_hit.astype(jnp.float32),
        precision=lax.Precision.HIGHEST,
    )
    teacher = lax.dot_general(
        combine,
        returned.astype(jnp.float32),
        (((0,), (0,)), ((), ())),
        precision=lax.Precision.HIGHEST,
    ).astype(jnp.bfloat16)

    teacher_far = swap(teacher, "c")
    pair = swap(teacher, "xl")
    order = jnp.stack([yh ^ xl, yh ^ xl ^ 1, core])
    pieces = product_pieces(order, teacher, teacher_far, pair, swap(pair, "c"), proj_block)
    pieces = [
        lax.ppermute(piece, ALL, permutation(home_target(step))).astype(jnp.float32)
        for step, piece in enumerate(pieces)
    ]
    target = pieces[0] + pieces[1]

    output_difference = student_out - target
    tokens_all = tok_rows * experts
    scale = 1.0 / math.sqrt(tokens_all)
    scaled = (output_difference * scale).astype(jnp.bfloat16)
    loss_here = jnp.sum(output_difference * output_difference)
    back_part = lax.dot_general(
        scaled, adapter_up_matrix, (((1,), (1,)), ((), ())), preferred_element_type=jnp.float32
    )
    back_low = (adapter_scale_factor * mp_sum(back_part)).astype(jnp.bfloat16)
    over_tokens = (((0,), (0,)), ((), ()))
    up_part = adapter_scale_factor * lax.dot_general(
        lowrank, scaled, over_tokens, preferred_element_type=jnp.float32
    )
    down_part = lax.dot_general(back_low, normed, over_tokens, preferred_element_type=jnp.float32)

    lanes = 128
    columns = up_part.shape[1]
    tiles = rank // 8 * (columns // lanes)
    first = lax.reduce_precision(loss_here, 8, 7)
    second = lax.reduce_precision(loss_here - first, 8, 7)
    third = loss_here - first - second
    lane = jnp.arange(lanes)
    loss_row = jnp.where(
        lane == 0, first, jnp.where(lane == 1, second, jnp.where(lane == 2, third, 0.0))
    )

    def to_tiles(value):
        value = value.astype(jnp.bfloat16).reshape(rank // 8, 8, columns // lanes, lanes)
        return value.transpose(0, 2, 1, 3).reshape(tiles, 8, lanes)

    def from_tiles(value):
        value = value.reshape(rank // 8, columns // lanes, 8, lanes).transpose(0, 2, 1, 3)
        return value.reshape(rank, columns).astype(jnp.float32)

    bundle = jnp.concatenate([to_tiles(up_part), to_tiles(down_part)])
    bundle = jnp.concatenate(
        [
            bundle[: 2 * experts].reshape(experts, 16, lanes),
            bundle[2 * experts :].reshape(experts, 4, lanes),
            jnp.broadcast_to(loss_row.astype(jnp.bfloat16), (experts, 4, lanes)),
        ],
        axis=1,
    )
    bundle = lax.all_to_all(bundle, DP, split_axis=0, concat_axis=0, tiled=True)
    summed = jnp.sum(bundle.astype(jnp.float32), axis=0)
    grads = jnp.broadcast_to(summed.astype(jnp.bfloat16), (experts, 24, lanes))
    grads = lax.all_to_all(grads, DP, split_axis=0, concat_axis=0, tiled=True)
    loss_row = summed[20:21]
    cross = [(i, 3 - i) for i in range(4)]
    loss_row = (loss_row + swap(loss_row, "c")) + (
        swap(loss_row, "yh") + lax.ppermute(loss_row, MP, cross)
    )
    loss = jnp.sum(loss_row) / (tokens_all * student_width)
    grads = jnp.concatenate(
        [
            grads[:, :16].reshape(2 * experts, 8, lanes),
            grads[:, 16:20].reshape(experts // 2, 8, lanes),
        ]
    )
    up_matrix_gradient = from_tiles(grads[:tiles])
    grad_a = from_tiles(grads[tiles:]).T
    return (target, grad_a, up_matrix_gradient, loss)


def solution(mesh):
    fine = Mesh(mesh.devices.reshape(SIZES), ALL)
    placed = (
        P(DP, MP),
        P(DP, None),
        P(DP, None),
        P(DP, None, MP),
        P(DP, None, MP),
        P(DP, MP, None),
        P(DP, MP),
        P(DP, MP),
        P(MP),
        P(MP, None),
        P(None, MP),
    )
    return jax.shard_map(
        body,
        mesh=fine,
        in_specs=placed,
        out_specs=(P(DP, MP), P(MP, None), P(None, MP), P()),
        check_vma=False,
    )
```

```python
import functools
import itertools
import math

import jax
import jax.numpy as jnp
from jax import lax
from jax.experimental import pallas as pl
from jax.experimental.pallas import tpu as pltpu
from jax.sharding import Mesh, PartitionSpec as P

route_scale = 2.5
adapter_scale_factor = 0.25
DP = ("yl", "z", "xh", "xl")
MP = ("yh", "c")
ALL = DP + MP
SIZES = (2, 8, 2, 2, 2, 2)


def permutation(target):
    places = list(itertools.product(*(range(size) for size in SIZES)))
    return [(place, places.index(target(*here))) for place, here in enumerate(places)]


def proj_target(step):
    return lambda yl, z, xh, xl, yh, c: (xl ^ (step & 1), z, xh ^ (step >> 1), yh, yl, c)


def home_target(step):
    return lambda yl, z, xh, xl, yh, c: (yl, z, xh, yh ^ step, xl, c)


def swap(value, axis):
    return lax.ppermute(value, axis, [(0, 1), (1, 0)])


def dot(a, b):
    return jnp.dot(a, b, preferred_element_type=jnp.float32)


def mp_sum(value):
    cross = lax.ppermute(value, MP, [(place, 3 - place) for place in range(4)])
    return (value + swap(value, "c")) + (swap(value, "yh") + cross)


def ordered(first, second, index):
    return jnp.where(
        index == 0, jnp.concatenate([first, second]), jnp.concatenate([second, first])
    )


def exchange_slots(rows):
    count, width = rows.shape
    rows = rows.reshape(64, count * width // (64 * 128), 128)
    return lax.all_to_all(rows, DP, split_axis=0, concat_axis=0, tiled=True).reshape(count, width)


def product_kernel(order_ref, own_ref, own_far_ref, pair_ref, pair_far_ref, block_ref, *refs):
    outs, near_rows, far_rows, total, held, arrived = refs[:2], *refs[2:]
    rows, width = own_ref.shape
    count, cut = held.shape[0], held.shape[2]
    copies = [
        pltpu.make_async_copy(
            block_ref.at[:, pl.ds(index * cut, cut)], held.at[index], arrived.at[index]
        )
        for index in range(count)
    ]
    for copy in copies:
        copy.start()
    near_rows[:rows] = own_ref[...]
    near_rows[rows:] = pair_ref[...]
    far_rows[:rows] = own_far_ref[...]
    far_rows[rows:] = pair_far_ref[...]
    core = order_ref[2]
    near = pl.ds(pl.multiple_of(core * width, 128), width)
    far = pl.ds(pl.multiple_of((1 - core) * width, 128), width)
    for index, copy in enumerate(copies):
        copy.wait()
        total[...] = dot(near_rows[...], held[index, near, :]) + dot(
            far_rows[...], held[index, far, :]
        )
        for step in range(2):
            here = pl.ds(pl.multiple_of(order_ref[step] * rows, 128), rows)
            outs[step][:, index * cut : (index + 1) * cut] = total[here, :].astype(jnp.bfloat16)


def product_pieces(order, own, own_far, pair, pair_far, block):
    rows, width = own.shape
    depth, wide = block.shape
    cut = 256
    vmem = pl.BlockSpec(memory_space=pltpu.VMEM)
    return pl.pallas_call(
        product_kernel,
        out_shape=[jax.ShapeDtypeStruct((rows, wide), jnp.bfloat16)] * 2,
        in_specs=[pl.BlockSpec(memory_space=pltpu.SMEM)]
        + [vmem] * 4
        + [pl.BlockSpec(memory_space=pltpu.HBM)],
        out_specs=[vmem] * 2,
        scratch_shapes=[
            pltpu.VMEM((2 * rows, width), jnp.bfloat16),
            pltpu.VMEM((2 * rows, width), jnp.bfloat16),
            pltpu.VMEM((2 * rows, cut), jnp.float32),
            pltpu.VMEM((wide // cut, depth, cut), jnp.bfloat16),
            pltpu.SemaphoreType.DMA((wide // cut,)),
        ],
        compiler_params=pltpu.CompilerParams(vmem_limit_bytes=24 * 1024 * 1024),
        cost_estimate=pl.CostEstimate(
            flops=4 * rows * depth * wide, bytes_accessed=6_000_000, transcendentals=0
        ),
    )(order, own, own_far, pair, pair_far, block)


def stats_kernel(student_ref, gain_ref, down_ref, out_ref):
    student = student_ref[...].astype(jnp.float32)
    scaled = (student * gain_ref[...].astype(jnp.float32)).astype(jnp.bfloat16)
    rank = down_ref.shape[0]
    out_ref[:, :rank] = lax.dot_general(
        scaled, down_ref[...], (((1,), (1,)), ((), ())), preferred_element_type=jnp.float32
    )
    total = jnp.sum(student * student, axis=-1, keepdims=True)
    out_ref[:, rank:] = jnp.broadcast_to(total, (student.shape[0], rank))


def student_kernel(width, stats_ref, student_ref, gain_ref, up_ref, low_ref, normed_ref, out_ref):
    rank = up_ref.shape[0]
    inverse = lax.rsqrt(stats_ref[:, rank : rank + 1] / width + 1e-06)
    low = (stats_ref[:, :rank] * inverse).astype(jnp.bfloat16)
    student = student_ref[...].astype(jnp.float32)
    low_ref[...] = low
    normed_ref[...] = (student * inverse * gain_ref[...].astype(jnp.float32)).astype(jnp.bfloat16)
    out_ref[...] = student + adapter_scale_factor * dot(low, up_ref[...])


def local_kernel(kernel, shapes, *args):
    vmem = pl.BlockSpec(memory_space=pltpu.VMEM)
    return pl.pallas_call(
        kernel,
        out_shape=shapes,
        in_specs=[vmem] * len(args),
        out_specs=jax.tree.map(lambda _: vmem, shapes),
        compiler_params=pltpu.CompilerParams(vmem_limit_bytes=16 * 1024 * 1024),
        cost_estimate=pl.CostEstimate(flops=100, bytes_accessed=100, transcendentals=0),
    )(*args)


def core_halves(core, width):
    return (
        pl.ds(pl.multiple_of(core * width, 128), width),
        pl.ds(pl.multiple_of((1 - core) * width, 128), width),
    )


def near_kernel(place_ref, own_ref, other_ref, gate_ref, up_ref, *refs):
    outs, held, arrived = refs[:2], refs[2], refs[3]
    depth = held.shape[1]
    here = pl.ds(pl.multiple_of(place_ref[0] * depth, 128), depth)
    copies = [
        pltpu.make_async_copy(weight.at[here, :], held.at[index], arrived.at[index])
        for index, weight in enumerate((gate_ref, up_ref))
    ]
    for copy in copies:
        copy.start()
    own, other = core_halves(place_ref[1], own_ref.shape[1])
    for index, copy in enumerate(copies):
        copy.wait()
        outs[index][...] = dot(own_ref[...], held[index, own, :]) + dot(
            other_ref[...], held[index, other, :]
        )


def expert_kernel(
    place_ref, gate_near_ref, up_near_ref, own_ref, other_ref, gate_ref, up_ref, down_ref, *refs
):
    outs, held, held_down, arrived = refs[:4], refs[4], refs[5], refs[6]
    depth, width = held.shape[1], own_ref.shape[1]
    yh, core = place_ref[0], place_ref[1]
    here = pl.ds(pl.multiple_of((1 - yh) * depth, 128), depth)
    copies = [
        pltpu.make_async_copy(weight.at[here, :], held.at[index], arrived.at[index])
        for index, weight in enumerate((gate_ref, up_ref))
    ]
    parts = (yh * 2 + core, yh * 2 + 1 - core, (1 - yh) * 2 + core, (1 - yh) * 2 + 1 - core)
    down_copies = [
        pltpu.make_async_copy(
            down_ref.at[:, pl.ds(pl.multiple_of(part * width, 128), width)],
            held_down.at[index],
            arrived.at[2 + index],
        )
        for index, part in enumerate(parts)
    ]
    for copy in copies + down_copies[::-1]:
        copy.start()
    own, other = core_halves(core, width)
    sums = []
    for index, near in enumerate((gate_near_ref, up_near_ref)):
        copies[index].wait()
        sums.append(
            near[...]
            + dot(own_ref[...], held[index, own, :])
            + dot(other_ref[...], held[index, other, :])
        )
    gate, up = sums
    hidden = (gate / (1.0 + jnp.exp(-gate)) * up).astype(jnp.bfloat16)
    for index in (3, 2, 1, 0):
        down_copies[index].wait()
        outs[index][...] = dot(hidden, held_down[index]).astype(jnp.bfloat16)


def expert_call(kernel, shapes, place, local, weights, scratch):
    vmem = pl.BlockSpec(memory_space=pltpu.VMEM)
    return pl.pallas_call(
        kernel,
        out_shape=shapes,
        in_specs=[pl.BlockSpec(memory_space=pltpu.SMEM)]
        + [vmem] * len(local)
        + [pl.BlockSpec(memory_space=pltpu.HBM)] * len(weights),
        out_specs=[vmem] * len(shapes),
        scratch_shapes=scratch,
        compiler_params=pltpu.CompilerParams(vmem_limit_bytes=32 * 1024 * 1024),
        cost_estimate=pl.CostEstimate(flops=100, bytes_accessed=100, transcendentals=0),
    )(place, *local, *weights)


def near_products(place, own, other, gate, up):
    depth, units = gate.shape[0] // 2, gate.shape[1]
    return expert_call(
        near_kernel,
        [jax.ShapeDtypeStruct((own.shape[0], units), jnp.float32)] * 2,
        place,
        (own, other),
        (gate, up),
        [pltpu.VMEM((2, depth, units), jnp.bfloat16), pltpu.SemaphoreType.DMA((2,))],
    )


def expert_products(place, near_gate, near_up, own, other, gate, up, down):
    depth, units = gate.shape[0] // 2, gate.shape[1]
    return expert_call(
        expert_kernel,
        [jax.ShapeDtypeStruct(own.shape, jnp.bfloat16)] * 4,
        place,
        (near_gate, near_up, own, other),
        (gate, up, down),
        [
            pltpu.VMEM((2, depth, units), jnp.bfloat16),
            pltpu.VMEM((4, units, own.shape[1]), jnp.bfloat16),
            pltpu.SemaphoreType.DMA((6,)),
        ],
    )


def body(
    tokens,
    routes,
    expert_gate_affinity,
    expert_gate_weight,
    expert_up_weight,
    expert_down_weight,
    proj,
    student_hidden_input,
    student_norm_weight,
    adapter_down_matrix,
    adapter_up_matrix,
):
    experts = 64
    mp_count = 4
    tok_rows, part_width = tokens.shape
    topk_count = routes.shape[1]
    assigned = tok_rows * topk_count
    capacity = 5
    slot_count = experts * capacity
    rank = adapter_up_matrix.shape[0]
    yl, xh, xl, yh, core = (lax.axis_index(name) for name in ("yl", "xh", "xl", "yh", "c"))
    mi = yh * 2 + core

    flat_routes = routes.reshape(assigned)
    onehot_e = (flat_routes[:, None] == jnp.arange(experts, dtype=jnp.int32)[None, :]).astype(
        jnp.int32
    )
    position = jnp.sum((jnp.cumsum(onehot_e, axis=0) - onehot_e) * onehot_e, axis=1)
    slot_index = flat_routes * capacity + position
    slot_hit = (jnp.arange(slot_count, dtype=jnp.int32)[:, None] == slot_index[None, :]).astype(
        jnp.bfloat16
    )
    token_hit = (
        jnp.arange(assigned, dtype=jnp.int32)[:, None] // topk_count
        == jnp.arange(tok_rows, dtype=jnp.int32)[None, :]
    ).astype(jnp.bfloat16)
    placing = dot(slot_hit, token_hit).astype(jnp.bfloat16)
    outgoing = dot(placing, tokens).astype(jnp.bfloat16)

    outgoing, proj = lax.optimization_barrier((outgoing, proj))
    arrived = exchange_slots(outgoing)

    blocks = [lax.ppermute(proj, ALL, permutation(proj_target(step))) for step in range(4)]
    proj_rows = ordered(ordered(*blocks[:2], yl), ordered(*blocks[2:], yl), xh)
    arrived, proj_rows = lax.optimization_barrier((arrived, proj_rows))
    proj_block = lax.all_gather(proj_rows, "z", axis=0, tiled=True)

    arrived_y = swap(arrived, "yh")
    arrived_c = swap(arrived, "c")

    gain = student_norm_weight.reshape(1, -1)
    stats = local_kernel(
        stats_kernel,
        jax.ShapeDtypeStruct((tok_rows, 2 * rank), jnp.float32),
        student_hidden_input,
        gain,
        adapter_down_matrix.T,
    )
    stats = stats + swap(stats, "c")
    near_gate, near_up = near_products(
        jnp.stack([yh, core]), arrived, arrived_c, expert_gate_weight[0], expert_up_weight[0]
    )
    arrived_y, stats, near_gate, near_up = lax.optimization_barrier(
        (arrived_y, stats, near_gate, near_up)
    )
    out_own, out_near, out_far, out_far_near = expert_products(
        jnp.stack([yh, core]),
        near_gate,
        near_up,
        arrived_y,
        swap(arrived_y, "c"),
        expert_gate_weight[0],
        expert_up_weight[0],
        expert_down_weight[0],
    )
    far = swap(out_far_near, "c")
    near = swap(out_near, "c")
    far = swap((out_far.astype(jnp.float32) + far.astype(jnp.float32)).astype(jnp.bfloat16), "yh")
    expert_out = (
        out_own.astype(jnp.float32)
        + near.astype(jnp.float32)
        + far.astype(jnp.float32)
    ).astype(jnp.bfloat16)
    returned = exchange_slots(expert_out)

    stats = stats + swap(stats, "yh")
    student_width = student_hidden_input.shape[1] * mp_count
    lowrank, normed, student_out = local_kernel(
        functools.partial(student_kernel, student_width),
        [
            jax.ShapeDtypeStruct((tok_rows, rank), jnp.bfloat16),
            jax.ShapeDtypeStruct(student_hidden_input.shape, jnp.bfloat16),
            jax.ShapeDtypeStruct(student_hidden_input.shape, jnp.float32),
        ],
        stats,
        student_hidden_input,
        gain,
        adapter_up_matrix,
    )
    returned, lowrank, normed, student_out, proj_block = lax.optimization_barrier(
        (returned, lowrank, normed, student_out, proj_block)
    )

    weights = (
        route_scale * expert_gate_affinity / jnp.sum(expert_gate_affinity, axis=-1, keepdims=True)
    )
    combine = jnp.dot(
        slot_hit.astype(jnp.float32) * weights.reshape(assigned)[None, :],
        token_hit.astype(jnp.float32),
        precision=lax.Precision.HIGHEST,
    )
    teacher = lax.dot_general(
        combine,
        returned.astype(jnp.float32),
        (((0,), (0,)), ((), ())),
        precision=lax.Precision.HIGHEST,
    ).astype(jnp.bfloat16)

    teacher_far = swap(teacher, "c")
    pair = swap(teacher, "xl")
    order = jnp.stack([yh ^ xl, yh ^ xl ^ 1, core])
    pieces = product_pieces(order, teacher, teacher_far, pair, swap(pair, "c"), proj_block)
    pieces = [
        lax.ppermute(piece, ALL, permutation(home_target(step))).astype(jnp.float32)
        for step, piece in enumerate(pieces)
    ]
    target = pieces[0] + pieces[1]

    output_difference = student_out - target
    tokens_all = tok_rows * experts
    scale = 1.0 / math.sqrt(tokens_all)
    scaled = (output_difference * scale).astype(jnp.bfloat16)
    loss_here = jnp.sum(output_difference * output_difference)
    back_part = lax.dot_general(
        scaled, adapter_up_matrix, (((1,), (1,)), ((), ())), preferred_element_type=jnp.float32
    )
    back_low = (adapter_scale_factor * mp_sum(back_part)).astype(jnp.bfloat16)
    over_tokens = (((0,), (0,)), ((), ()))
    up_part = adapter_scale_factor * lax.dot_general(
        lowrank, scaled, over_tokens, preferred_element_type=jnp.float32
    )
    down_part = lax.dot_general(back_low, normed, over_tokens, preferred_element_type=jnp.float32)

    lanes = 128
    columns = up_part.shape[1]
    tiles = rank // 8 * (columns // lanes)
    first = lax.reduce_precision(loss_here, 8, 7)
    second = lax.reduce_precision(loss_here - first, 8, 7)
    third = loss_here - first - second
    lane = jnp.arange(lanes)
    loss_row = jnp.where(
        lane == 0, first, jnp.where(lane == 1, second, jnp.where(lane == 2, third, 0.0))
    )

    def to_tiles(value):
        value = value.astype(jnp.bfloat16).reshape(rank // 8, 8, columns // lanes, lanes)
        return value.transpose(0, 2, 1, 3).reshape(tiles, 8, lanes)

    def from_tiles(value):
        value = value.reshape(rank // 8, columns // lanes, 8, lanes).transpose(0, 2, 1, 3)
        return value.reshape(rank, columns).astype(jnp.float32)

    bundle = jnp.concatenate([to_tiles(up_part), to_tiles(down_part)])
    bundle = jnp.concatenate(
        [
            bundle[: 2 * experts].reshape(experts, 16, lanes),
            bundle[2 * experts :].reshape(experts, 4, lanes),
            jnp.broadcast_to(loss_row.astype(jnp.bfloat16), (experts, 4, lanes)),
        ],
        axis=1,
    )
    bundle = lax.all_to_all(bundle, DP, split_axis=0, concat_axis=0, tiled=True)
    summed = jnp.sum(bundle.astype(jnp.float32), axis=0)
    grads = jnp.broadcast_to(summed.astype(jnp.bfloat16), (experts, 24, lanes))
    grads = lax.all_to_all(grads, DP, split_axis=0, concat_axis=0, tiled=True)
    loss = jnp.sum(mp_sum(summed[20:21])) / (tokens_all * student_width)
    grads = jnp.concatenate(
        [
            grads[:, :16].reshape(2 * experts, 8, lanes),
            grads[:, 16:20].reshape(experts // 2, 8, lanes),
        ]
    )
    up_matrix_gradient = from_tiles(grads[:tiles])
    grad_a = from_tiles(grads[tiles:]).T
    return (target, grad_a, up_matrix_gradient, loss)


def solution(mesh):
    fine = Mesh(mesh.devices.reshape(SIZES), ALL)
    placed = (
        P(DP, MP),
        P(DP, None),
        P(DP, None),
        P(DP, None, MP),
        P(DP, None, MP),
        P(DP, MP, None),
        P(DP, MP),
        P(DP, MP),
        P(MP),
        P(MP, None),
        P(None, MP),
    )
    return jax.shard_map(
        body,
        mesh=fine,
        in_specs=placed,
        out_specs=(P(DP, MP), P(MP, None), P(None, MP), P()),
        check_vma=False,
    )
```

```python
import functools
import itertools
import math

import jax
import jax.numpy as jnp
from jax import lax
from jax.experimental import pallas as pl
from jax.experimental.pallas import tpu as pltpu
from jax.sharding import Mesh, PartitionSpec as P

route_scale = 2.5
adapter_scale_factor = 0.25
DP = ("yl", "z", "xh", "xl")
MP = ("yh", "c")
ALL = DP + MP
SIZES = (2, 8, 2, 2, 2, 2)


def permutation(target):
    places = list(itertools.product(*(range(size) for size in SIZES)))
    return [(place, places.index(target(*here))) for place, here in enumerate(places)]


def proj_target(yl, z, xh, xl, yh, c):
    return (xl, z, xh, yh, yl, c)


def home_target(step):
    return lambda yl, z, xh, xl, yh, c: (yl, z, xh, yh ^ step, xl, c)


def swap(value, axis):
    return lax.ppermute(value, axis, [(0, 1), (1, 0)])


def dot(a, b):
    return jnp.dot(a, b, preferred_element_type=jnp.float32)


def mp_sum(value):
    cross = lax.ppermute(value, MP, [(place, 3 - place) for place in range(4)])
    return (value + swap(value, "c")) + (swap(value, "yh") + cross)


def ordered(first, second, index):
    return jnp.where(
        index == 0, jnp.concatenate([first, second]), jnp.concatenate([second, first])
    )


def exchange_slots(rows):
    count, width = rows.shape
    rows = rows.reshape(64, count * width // (64 * 128), 128)
    return lax.all_to_all(rows, DP, split_axis=0, concat_axis=0, tiled=True).reshape(count, width)


def product_kernel(order_ref, own_ref, own_far_ref, pair_ref, pair_far_ref, block_ref, *refs):
    outs, near_rows, far_rows, total, held, arrived = refs[:2], *refs[2:]
    rows, width = own_ref.shape
    count, cut = held.shape[0], held.shape[2]
    copies = [
        pltpu.make_async_copy(
            block_ref.at[:, pl.ds(index * cut, cut)], held.at[index], arrived.at[index]
        )
        for index in range(count)
    ]
    for copy in copies:
        copy.start()
    near_rows[:rows] = own_ref[...]
    near_rows[rows:] = pair_ref[...]
    far_rows[:rows] = own_far_ref[...]
    far_rows[rows:] = pair_far_ref[...]
    core = order_ref[2]
    near = pl.ds(pl.multiple_of(core * width, 128), width)
    far = pl.ds(pl.multiple_of((1 - core) * width, 128), width)
    for index, copy in enumerate(copies):
        copy.wait()
        total[...] = dot(near_rows[...], held[index, near, :]) + dot(
            far_rows[...], held[index, far, :]
        )
        for step in range(2):
            here = pl.ds(pl.multiple_of(order_ref[step] * rows, 128), rows)
            outs[step][:, index * cut : (index + 1) * cut] = total[here, :].astype(jnp.bfloat16)


def product_pieces(order, own, own_far, pair, pair_far, block):
    rows, width = own.shape
    depth, wide = block.shape
    cut = 256
    vmem = pl.BlockSpec(memory_space=pltpu.VMEM)
    return pl.pallas_call(
        product_kernel,
        out_shape=[jax.ShapeDtypeStruct((rows, wide), jnp.bfloat16)] * 2,
        in_specs=[pl.BlockSpec(memory_space=pltpu.SMEM)]
        + [vmem] * 4
        + [pl.BlockSpec(memory_space=pltpu.HBM)],
        out_specs=[vmem] * 2,
        scratch_shapes=[
            pltpu.VMEM((2 * rows, width), jnp.bfloat16),
            pltpu.VMEM((2 * rows, width), jnp.bfloat16),
            pltpu.VMEM((2 * rows, cut), jnp.float32),
            pltpu.VMEM((wide // cut, depth, cut), jnp.bfloat16),
            pltpu.SemaphoreType.DMA((wide // cut,)),
        ],
        compiler_params=pltpu.CompilerParams(vmem_limit_bytes=61 * 1024 * 1024),
        cost_estimate=pl.CostEstimate(
            flops=4 * rows * depth * wide, bytes_accessed=6_000_000, transcendentals=0
        ),
    )(order, own, own_far, pair, pair_far, block)


def stats_kernel(student_ref, gain_ref, down_ref, out_ref):
    student = student_ref[...].astype(jnp.float32)
    scaled = (student * gain_ref[...].astype(jnp.float32)).astype(jnp.bfloat16)
    rank = down_ref.shape[0]
    out_ref[:, :rank] = lax.dot_general(
        scaled, down_ref[...], (((1,), (1,)), ((), ())), preferred_element_type=jnp.float32
    )
    total = jnp.sum(student * student, axis=-1, keepdims=True)
    out_ref[:, rank:] = jnp.broadcast_to(total, (student.shape[0], rank))


def student_kernel(width, stats_ref, student_ref, gain_ref, up_ref, low_ref, normed_ref, out_ref):
    rank = up_ref.shape[0]
    inverse = lax.rsqrt(stats_ref[:, rank : rank + 1] / width + 1e-06)
    low = (stats_ref[:, :rank] * inverse).astype(jnp.bfloat16)
    student = student_ref[...].astype(jnp.float32)
    low_ref[...] = low
    normed_ref[...] = (student * inverse * gain_ref[...].astype(jnp.float32)).astype(jnp.bfloat16)
    out_ref[...] = student + adapter_scale_factor * dot(low, up_ref[...])


def local_kernel(kernel, shapes, *args):
    vmem = pl.BlockSpec(memory_space=pltpu.VMEM)
    return pl.pallas_call(
        kernel,
        out_shape=shapes,
        in_specs=[vmem] * len(args),
        out_specs=jax.tree.map(lambda _: vmem, shapes),
        compiler_params=pltpu.CompilerParams(vmem_limit_bytes=16 * 1024 * 1024),
        cost_estimate=pl.CostEstimate(flops=100, bytes_accessed=100, transcendentals=0),
    )(*args)


def core_halves(core, width):
    return (
        pl.ds(pl.multiple_of(core * width, 128), width),
        pl.ds(pl.multiple_of((1 - core) * width, 128), width),
    )


def near_kernel(place_ref, own_ref, other_ref, gate_ref, up_ref, *refs):
    outs, held, arrived = refs[:2], refs[2], refs[3]
    depth = held.shape[1]
    here = pl.ds(pl.multiple_of(place_ref[0] * depth, 128), depth)
    copies = [
        pltpu.make_async_copy(weight.at[here, :], held.at[index], arrived.at[index])
        for index, weight in enumerate((gate_ref, up_ref))
    ]
    for copy in copies:
        copy.start()
    own, other = core_halves(place_ref[1], own_ref.shape[1])
    for index, copy in enumerate(copies):
        copy.wait()
        outs[index][...] = dot(own_ref[...], held[index, own, :]) + dot(
            other_ref[...], held[index, other, :]
        )


def expert_kernel(
    place_ref, gate_near_ref, up_near_ref, own_ref, other_ref, gate_ref, up_ref, down_ref, *refs
):
    outs, held, held_down, arrived = refs[:4], refs[4], refs[5], refs[6]
    depth, width = held.shape[1], own_ref.shape[1]
    yh, core = place_ref[0], place_ref[1]
    here = pl.ds(pl.multiple_of((1 - yh) * depth, 128), depth)
    copies = [
        pltpu.make_async_copy(weight.at[here, :], held.at[index], arrived.at[index])
        for index, weight in enumerate((gate_ref, up_ref))
    ]
    parts = (yh * 2 + core, yh * 2 + 1 - core, (1 - yh) * 2 + core, (1 - yh) * 2 + 1 - core)
    down_copies = [
        pltpu.make_async_copy(
            down_ref.at[:, pl.ds(pl.multiple_of(part * width, 128), width)],
            held_down.at[index],
            arrived.at[2 + index],
        )
        for index, part in enumerate(parts)
    ]
    for copy in copies + down_copies[::-1]:
        copy.start()
    own, other = core_halves(core, width)
    sums = []
    for index, near in enumerate((gate_near_ref, up_near_ref)):
        copies[index].wait()
        sums.append(
            near[...]
            + dot(own_ref[...], held[index, own, :])
            + dot(other_ref[...], held[index, other, :])
        )
    gate, up = sums
    hidden = (gate / (1.0 + jnp.exp(-gate)) * up).astype(jnp.bfloat16)
    for index in (3, 2, 1, 0):
        down_copies[index].wait()
        outs[index][...] = dot(hidden, held_down[index]).astype(jnp.bfloat16)


def expert_call(kernel, shapes, place, local, weights, scratch):
    vmem = pl.BlockSpec(memory_space=pltpu.VMEM)
    return pl.pallas_call(
        kernel,
        out_shape=shapes,
        in_specs=[pl.BlockSpec(memory_space=pltpu.SMEM)]
        + [vmem] * len(local)
        + [pl.BlockSpec(memory_space=pltpu.HBM)] * len(weights),
        out_specs=[vmem] * len(shapes),
        scratch_shapes=scratch,
        compiler_params=pltpu.CompilerParams(vmem_limit_bytes=61 * 1024 * 1024),
        cost_estimate=pl.CostEstimate(flops=100, bytes_accessed=100, transcendentals=0),
    )(place, *local, *weights)


def near_products(place, own, other, gate, up):
    depth, units = gate.shape[0] // 2, gate.shape[1]
    return expert_call(
        near_kernel,
        [jax.ShapeDtypeStruct((own.shape[0], units), jnp.float32)] * 2,
        place,
        (own, other),
        (gate, up),
        [pltpu.VMEM((2, depth, units), jnp.bfloat16), pltpu.SemaphoreType.DMA((2,))],
    )


def expert_products(place, near_gate, near_up, own, other, gate, up, down):
    depth, units = gate.shape[0] // 2, gate.shape[1]
    return expert_call(
        expert_kernel,
        [jax.ShapeDtypeStruct(own.shape, jnp.bfloat16)] * 4,
        place,
        (near_gate, near_up, own, other),
        (gate, up, down),
        [
            pltpu.VMEM((2, depth, units), jnp.bfloat16),
            pltpu.VMEM((4, units, own.shape[1]), jnp.bfloat16),
            pltpu.SemaphoreType.DMA((6,)),
        ],
    )


def body(
    tokens,
    routes,
    expert_gate_affinity,
    expert_gate_weight,
    expert_up_weight,
    expert_down_weight,
    proj,
    student_hidden_input,
    student_norm_weight,
    adapter_down_matrix,
    adapter_up_matrix,
):
    experts = 64
    mp_count = 4
    tok_rows, part_width = tokens.shape
    topk_count = routes.shape[1]
    assigned = tok_rows * topk_count
    capacity = 5
    slot_count = experts * capacity
    rank = adapter_up_matrix.shape[0]
    yl, xh, xl, yh, core = (lax.axis_index(name) for name in ("yl", "xh", "xl", "yh", "c"))
    mi = yh * 2 + core

    flat_routes = routes.reshape(assigned)
    onehot_e = (flat_routes[:, None] == jnp.arange(experts, dtype=jnp.int32)[None, :]).astype(
        jnp.int32
    )
    position = jnp.sum((jnp.cumsum(onehot_e, axis=0) - onehot_e) * onehot_e, axis=1)
    slot_index = flat_routes * capacity + position
    slot_hit = (jnp.arange(slot_count, dtype=jnp.int32)[:, None] == slot_index[None, :]).astype(
        jnp.bfloat16
    )
    token_hit = (
        jnp.arange(assigned, dtype=jnp.int32)[:, None] // topk_count
        == jnp.arange(tok_rows, dtype=jnp.int32)[None, :]
    ).astype(jnp.bfloat16)
    placing = dot(slot_hit, token_hit).astype(jnp.bfloat16)
    outgoing = dot(placing, tokens).astype(jnp.bfloat16)

    outgoing, proj = lax.optimization_barrier((outgoing, proj))
    arrived = exchange_slots(outgoing)

    proj_rows = lax.ppermute(proj, ALL, permutation(proj_target))
    proj_rows = ordered(proj_rows, swap(proj_rows, "yl"), yl)
    arrived, proj_rows = lax.optimization_barrier((arrived, proj_rows))

    arrived_y = swap(arrived, "yh")
    arrived_c = swap(arrived, "c")
    proj_rows = ordered(proj_rows, swap(proj_rows, "xh"), xh)
    proj_block = lax.all_gather(proj_rows, "z", axis=0, tiled=True)

    gain = student_norm_weight.reshape(1, -1)
    stats = local_kernel(
        stats_kernel,
        jax.ShapeDtypeStruct((tok_rows, 2 * rank), jnp.float32),
        student_hidden_input,
        gain,
        adapter_down_matrix.T,
    )
    stats = stats + swap(stats, "c")
    near_gate, near_up = near_products(
        jnp.stack([yh, core]), arrived, arrived_c, expert_gate_weight[0], expert_up_weight[0]
    )
    arrived_y, stats, near_gate, near_up = lax.optimization_barrier(
        (arrived_y, stats, near_gate, near_up)
    )
    out_own, out_near, out_far, out_far_near = expert_products(
        jnp.stack([yh, core]),
        near_gate,
        near_up,
        arrived_y,
        swap(arrived_y, "c"),
        expert_gate_weight[0],
        expert_up_weight[0],
        expert_down_weight[0],
    )
    far = swap(out_far_near, "c")
    near = swap(out_near, "c")
    far = swap((out_far.astype(jnp.float32) + far.astype(jnp.float32)).astype(jnp.bfloat16), "yh")
    expert_out = (
        out_own.astype(jnp.float32)
        + near.astype(jnp.float32)
        + far.astype(jnp.float32)
    ).astype(jnp.bfloat16)
    returned = exchange_slots(expert_out)

    stats = stats + swap(stats, "yh")
    student_width = student_hidden_input.shape[1] * mp_count
    lowrank, normed, student_out = local_kernel(
        functools.partial(student_kernel, student_width),
        [
            jax.ShapeDtypeStruct((tok_rows, rank), jnp.bfloat16),
            jax.ShapeDtypeStruct(student_hidden_input.shape, jnp.bfloat16),
            jax.ShapeDtypeStruct(student_hidden_input.shape, jnp.float32),
        ],
        stats,
        student_hidden_input,
        gain,
        adapter_up_matrix,
    )
    returned, lowrank, normed, student_out, proj_block = lax.optimization_barrier(
        (returned, lowrank, normed, student_out, proj_block)
    )

    weights = (
        route_scale * expert_gate_affinity / jnp.sum(expert_gate_affinity, axis=-1, keepdims=True)
    )
    combine = jnp.dot(
        slot_hit.astype(jnp.float32) * weights.reshape(assigned)[None, :],
        token_hit.astype(jnp.float32),
        precision=lax.Precision.HIGHEST,
    )
    teacher = lax.dot_general(
        combine,
        returned.astype(jnp.float32),
        (((0,), (0,)), ((), ())),
        precision=lax.Precision.HIGHEST,
    ).astype(jnp.bfloat16)

    teacher_far = swap(teacher, "c")
    pair = swap(teacher, "xl")
    order = jnp.stack([yh ^ xl, yh ^ xl ^ 1, core])
    pieces = product_pieces(order, teacher, teacher_far, pair, swap(pair, "c"), proj_block)
    pieces = [
        lax.ppermute(piece, ALL, permutation(home_target(step))).astype(jnp.float32)
        for step, piece in enumerate(pieces)
    ]
    target = pieces[0] + pieces[1]

    output_difference = student_out - target
    tokens_all = tok_rows * experts
    scale = 1.0 / math.sqrt(tokens_all)
    scaled = (output_difference * scale).astype(jnp.bfloat16)
    loss_here = jnp.sum(output_difference * output_difference)
    back_part = lax.dot_general(
        scaled, adapter_up_matrix, (((1,), (1,)), ((), ())), preferred_element_type=jnp.float32
    )
    back_low = (adapter_scale_factor * mp_sum(back_part)).astype(jnp.bfloat16)
    over_tokens = (((0,), (0,)), ((), ()))
    up_part = adapter_scale_factor * lax.dot_general(
        lowrank, scaled, over_tokens, preferred_element_type=jnp.float32
    )
    down_part = lax.dot_general(back_low, normed, over_tokens, preferred_element_type=jnp.float32)

    lanes = 128
    columns = up_part.shape[1]
    tiles = rank // 8 * (columns // lanes)

    def to_tiles(value):
        value = value.astype(jnp.bfloat16).reshape(rank // 8, 8, columns // lanes, lanes)
        return value.transpose(0, 2, 1, 3).reshape(tiles, 8, lanes)

    def from_tiles(value):
        value = value.reshape(rank // 8, columns // lanes, 8, lanes).transpose(0, 2, 1, 3)
        return value.reshape(rank, columns).astype(jnp.float32)

    def to_row(total):
        first = lax.reduce_precision(total, 8, 7)
        second = lax.reduce_precision(total - first, 8, 7)
        third = total - first - second
        lane = jnp.arange(lanes)
        row = jnp.where(
            lane == 0, first, jnp.where(lane == 1, second, jnp.where(lane == 2, third, 0.0))
        )
        return row.astype(jnp.bfloat16)

    def exchange(value, axes):
        return lax.all_to_all(value, axes, split_axis=0, concat_axis=0, tiled=True)

    along_x, across = ("xh", "xl"), ("yl", "z")
    quarter = 2 * tiles // 4
    bundle = jnp.concatenate([to_tiles(up_part), to_tiles(down_part)])
    bundle = jnp.concatenate(
        [
            bundle.reshape(4, quarter, 8, lanes),
            jnp.broadcast_to(to_row(loss_here), (4, 1, 8, lanes)),
        ],
        axis=1,
    )
    bundle = jnp.sum(exchange(bundle, along_x).astype(jnp.float32), axis=0)
    loss_x = jnp.sum(bundle[quarter, 0])
    bundle = bundle[:quarter].astype(jnp.bfloat16)
    bundle = jnp.concatenate(
        [
            bundle[:32].reshape(16, 16, lanes),
            bundle[32:].reshape(16, 4, lanes),
            jnp.broadcast_to(to_row(loss_x), (16, 4, lanes)),
        ],
        axis=1,
    )
    summed = jnp.sum(exchange(bundle, across).astype(jnp.float32), axis=0)
    grads = exchange(jnp.broadcast_to(summed.astype(jnp.bfloat16), (16, 24, lanes)), across)
    loss = jnp.sum(mp_sum(summed[20:21])) / (tokens_all * student_hidden_input.shape[1] * mp_count)
    grads = jnp.concatenate(
        [grads[:, :16].reshape(32, 8, lanes), grads[:, 16:20].reshape(8, 8, lanes)]
    )
    grads = exchange(jnp.broadcast_to(grads, (4, quarter, 8, lanes)), along_x)
    grads = grads.reshape(2 * tiles, 8, lanes)
    up_matrix_gradient = from_tiles(grads[:tiles])
    grad_a = from_tiles(grads[tiles:]).T
    return (target, grad_a, up_matrix_gradient, loss)


def solution(mesh):
    fine = Mesh(mesh.devices.reshape(SIZES), ALL)
    placed = (
        P(DP, MP),
        P(DP, None),
        P(DP, None),
        P(DP, None, MP),
        P(DP, None, MP),
        P(DP, MP, None),
        P(DP, MP),
        P(DP, MP),
        P(MP),
        P(MP, None),
        P(None, MP),
    )
    return jax.shard_map(
        body,
        mesh=fine,
        in_specs=placed,
        out_specs=(P(DP, MP), P(MP, None), P(None, MP), P()),
        check_vma=False,
    )
```

```python
import functools
import itertools
import math

import jax
import jax.numpy as jnp
from jax import lax
from jax.experimental import pallas as pl
from jax.experimental.pallas import tpu as pltpu
from jax.sharding import Mesh, PartitionSpec as P

route_scale = 2.5
adapter_scale_factor = 0.25
DP = ("yl", "z", "xh", "xl")
MP = ("yh", "c")
ALL = DP + MP
SIZES = (2, 8, 2, 2, 2, 2)


def permutation(target):
    places = list(itertools.product(*(range(size) for size in SIZES)))
    return [(place, places.index(target(*here))) for place, here in enumerate(places)]


def proj_target(step):
    return lambda yl, z, xh, xl, yh, c: (xl ^ step, z, xh, yh, yl, c)


def home_target(step):
    return lambda yl, z, xh, xl, yh, c: (yl, z, xh, yh ^ step, xl, c)


def swap(value, axis):
    return lax.ppermute(value, axis, [(0, 1), (1, 0)])


def dot(a, b):
    return jnp.dot(a, b, preferred_element_type=jnp.float32)


def mp_sum(value):
    cross = lax.ppermute(value, MP, [(place, 3 - place) for place in range(4)])
    return (value + swap(value, "c")) + (swap(value, "yh") + cross)


def ordered(first, second, index):
    return jnp.where(
        index == 0, jnp.concatenate([first, second]), jnp.concatenate([second, first])
    )


def exchange_slots(rows):
    count, width = rows.shape
    rows = rows.reshape(64, count * width // (64 * 128), 128)
    return lax.all_to_all(rows, DP, split_axis=0, concat_axis=0, tiled=True).reshape(count, width)


def product_kernel(order_ref, own_ref, own_far_ref, pair_ref, pair_far_ref, block_ref, *refs):
    outs, near_rows, far_rows, total = refs[:2], *refs[2:]
    rows, width = own_ref.shape
    near_rows[:rows] = own_ref[...]
    near_rows[rows:] = pair_ref[...]
    far_rows[:rows] = own_far_ref[...]
    far_rows[rows:] = pair_far_ref[...]
    core = order_ref[2]
    near = pl.ds(pl.multiple_of(core * width, 128), width)
    far = pl.ds(pl.multiple_of((1 - core) * width, 128), width)
    cut = total.shape[1]
    for start in range(0, block_ref.shape[1], cut):
        columns = slice(start, start + cut)
        total[...] = dot(near_rows[...], block_ref[near, columns]) + dot(
            far_rows[...], block_ref[far, columns]
        )
        for step in range(2):
            here = pl.ds(pl.multiple_of(order_ref[step] * rows, 128), rows)
            outs[step][:, columns] = total[here, :].astype(jnp.bfloat16)


def product_pieces(order, own, own_far, pair, pair_far, block):
    rows, width = own.shape
    depth, wide = block.shape
    vmem = pl.BlockSpec(memory_space=pltpu.VMEM)
    return pl.pallas_call(
        product_kernel,
        out_shape=[jax.ShapeDtypeStruct((rows, wide), jnp.bfloat16)] * 2,
        in_specs=[pl.BlockSpec(memory_space=pltpu.SMEM)] + [vmem] * 5,
        out_specs=[vmem] * 2,
        scratch_shapes=[
            pltpu.VMEM((2 * rows, width), jnp.bfloat16),
            pltpu.VMEM((2 * rows, width), jnp.bfloat16),
            pltpu.VMEM((2 * rows, 640), jnp.float32),
        ],
        compiler_params=pltpu.CompilerParams(vmem_limit_bytes=24 * 1024 * 1024),
        cost_estimate=pl.CostEstimate(flops=100, bytes_accessed=100, transcendentals=0),
    )(order, own, own_far, pair, pair_far, block)


def stats_kernel(student_ref, gain_ref, down_ref, out_ref):
    student = student_ref[...].astype(jnp.float32)
    scaled = (student * gain_ref[...].astype(jnp.float32)).astype(jnp.bfloat16)
    rank = down_ref.shape[0]
    out_ref[:, :rank] = lax.dot_general(
        scaled, down_ref[...], (((1,), (1,)), ((), ())), preferred_element_type=jnp.float32
    )
    total = jnp.sum(student * student, axis=-1, keepdims=True)
    out_ref[:, rank:] = jnp.broadcast_to(total, (student.shape[0], rank))


def student_kernel(width, stats_ref, student_ref, gain_ref, up_ref, block_ref, *outs):
    low_ref, normed_ref, out_ref = outs
    rank = up_ref.shape[0]
    inverse = lax.rsqrt(stats_ref[:, rank : rank + 1] / width + 1e-06)
    low = (stats_ref[:, :rank] * inverse).astype(jnp.bfloat16)
    student = student_ref[...].astype(jnp.float32)
    low_ref[...] = low
    normed_ref[...] = (student * inverse * gain_ref[...].astype(jnp.float32)).astype(jnp.bfloat16)
    out_ref[...] = student + adapter_scale_factor * dot(low, up_ref[...])


def local_kernel(kernel, shapes, *args):
    vmem = pl.BlockSpec(memory_space=pltpu.VMEM)
    return pl.pallas_call(
        kernel,
        out_shape=shapes,
        in_specs=[vmem] * len(args),
        out_specs=jax.tree.map(lambda _: vmem, shapes),
        compiler_params=pltpu.CompilerParams(vmem_limit_bytes=16 * 1024 * 1024),
        cost_estimate=pl.CostEstimate(flops=100, bytes_accessed=100, transcendentals=0),
    )(*args)


def half_rows(ref, half, core, width):
    start = half * 2 * width
    own = pl.ds(pl.multiple_of(start + core * width, 128), width)
    other = pl.ds(pl.multiple_of(start + (1 - core) * width, 128), width)
    return ref[own, :], ref[other, :]


def near_kernel(place_ref, own_ref, other_ref, gate_ref, up_ref, down_ref, *outs):
    for out_ref, weight_ref in zip(outs, (gate_ref, up_ref)):
        own, other = half_rows(weight_ref, place_ref[0], place_ref[1], own_ref.shape[1])
        out_ref[...] = dot(own_ref[...], own) + dot(other_ref[...], other)


def expert_kernel(
    place_ref, gate_near_ref, up_near_ref, own_ref, other_ref, gate_ref, up_ref, down_ref, *outs
):
    yh, core, width = place_ref[0], place_ref[1], own_ref.shape[1]
    sums = []
    for near, weight_ref in ((gate_near_ref, gate_ref), (up_near_ref, up_ref)):
        own, other = half_rows(weight_ref, 1 - yh, core, width)
        sums.append(near[...] + dot(own_ref[...], own) + dot(other_ref[...], other))
    gate, up = sums
    hidden = (gate / (1.0 + jnp.exp(-gate)) * up).astype(jnp.bfloat16)
    parts = (yh * 2 + core, yh * 2 + 1 - core, (1 - yh) * 2 + core, (1 - yh) * 2 + 1 - core)
    for out_ref, part in zip(outs, parts):
        columns = pl.ds(pl.multiple_of(part * width, 128), width)
        out_ref[...] = dot(hidden, down_ref[:, columns]).astype(jnp.bfloat16)


def expert_call(kernel, shapes, place, *args):
    vmem = pl.BlockSpec(memory_space=pltpu.VMEM)
    return pl.pallas_call(
        kernel,
        out_shape=shapes,
        in_specs=[pl.BlockSpec(memory_space=pltpu.SMEM)] + [vmem] * len(args),
        out_specs=[vmem] * len(shapes),
        compiler_params=pltpu.CompilerParams(vmem_limit_bytes=32 * 1024 * 1024),
        cost_estimate=pl.CostEstimate(flops=100, bytes_accessed=100, transcendentals=0),
    )(place, *args)


def body(
    tokens,
    routes,
    expert_gate_affinity,
    expert_gate_weight,
    expert_up_weight,
    expert_down_weight,
    proj,
    student_hidden_input,
    student_norm_weight,
    adapter_down_matrix,
    adapter_up_matrix,
):
    experts = 64
    mp_count = 4
    tok_rows, part_width = tokens.shape
    topk_count = routes.shape[1]
    assigned = tok_rows * topk_count
    capacity = 5
    slot_count = experts * capacity
    rank = adapter_up_matrix.shape[0]
    yl, xh, xl, yh, core = (lax.axis_index(name) for name in ("yl", "xh", "xl", "yh", "c"))
    mi = yh * 2 + core

    flat_routes = routes.reshape(assigned)
    onehot_e = (flat_routes[:, None] == jnp.arange(experts, dtype=jnp.int32)[None, :]).astype(
        jnp.int32
    )
    position = jnp.sum((jnp.cumsum(onehot_e, axis=0) - onehot_e) * onehot_e, axis=1)
    slot_index = flat_routes * capacity + position
    slot_hit = (jnp.arange(slot_count, dtype=jnp.int32)[:, None] == slot_index[None, :]).astype(
        jnp.bfloat16
    )
    token_hit = (
        jnp.arange(assigned, dtype=jnp.int32)[:, None] // topk_count
        == jnp.arange(tok_rows, dtype=jnp.int32)[None, :]
    ).astype(jnp.bfloat16)
    placing = dot(slot_hit, token_hit).astype(jnp.bfloat16)
    outgoing = dot(placing, tokens).astype(jnp.bfloat16)

    outgoing, proj = lax.optimization_barrier((outgoing, proj))
    arrived = exchange_slots(outgoing)

    blocks = [lax.ppermute(proj, ALL, permutation(proj_target(step))) for step in range(2)]
    proj_rows = ordered(*blocks, yl)
    proj_rows = ordered(proj_rows, swap(proj_rows, "xh"), xh)
    arrived, proj_rows = lax.optimization_barrier((arrived, proj_rows))
    proj_block = lax.all_gather(proj_rows, "z", axis=0, tiled=True)

    arrived_y = swap(arrived, "yh")
    arrived_c = swap(arrived, "c")

    gain = student_norm_weight.reshape(1, -1)
    stats = local_kernel(
        stats_kernel,
        jax.ShapeDtypeStruct((tok_rows, 2 * rank), jnp.float32),
        student_hidden_input,
        gain,
        adapter_down_matrix.T,
    )
    stats = stats + swap(stats, "c")
    place = jnp.stack([yh, core])
    expert_weights = (expert_gate_weight[0], expert_up_weight[0], expert_down_weight[0])
    units = expert_weights[0].shape[1]
    near_gate, near_up = expert_call(
        near_kernel,
        [jax.ShapeDtypeStruct((slot_count, units), jnp.float32)] * 2,
        place,
        arrived,
        arrived_c,
        *expert_weights,
    )
    arrived_y, stats, near_gate, near_up = lax.optimization_barrier(
        (arrived_y, stats, near_gate, near_up)
    )
    out_own, out_near, out_far, out_far_near = expert_call(
        expert_kernel,
        [jax.ShapeDtypeStruct(arrived.shape, jnp.bfloat16)] * 4,
        place,
        near_gate,
        near_up,
        arrived_y,
        swap(arrived_y, "c"),
        *expert_weights,
    )
    far = swap(out_far_near, "c")
    near = swap(out_near, "c")
    far = swap((out_far.astype(jnp.float32) + far.astype(jnp.float32)).astype(jnp.bfloat16), "yh")
    expert_out = (
        out_own.astype(jnp.float32)
        + near.astype(jnp.float32)
        + far.astype(jnp.float32)
    ).astype(jnp.bfloat16)
    returned = exchange_slots(expert_out)

    stats = stats + swap(stats, "yh")
    student_width = student_hidden_input.shape[1] * mp_count
    lowrank, normed, student_out = local_kernel(
        functools.partial(student_kernel, student_width),
        [
            jax.ShapeDtypeStruct((tok_rows, rank), jnp.bfloat16),
            jax.ShapeDtypeStruct(student_hidden_input.shape, jnp.bfloat16),
            jax.ShapeDtypeStruct(student_hidden_input.shape, jnp.float32),
        ],
        stats,
        student_hidden_input,
        gain,
        adapter_up_matrix,
        proj_block,
    )
    returned, lowrank, normed, student_out = lax.optimization_barrier(
        (returned, lowrank, normed, student_out)
    )

    weights = (
        route_scale * expert_gate_affinity / jnp.sum(expert_gate_affinity, axis=-1, keepdims=True)
    )
    combine = jnp.dot(
        slot_hit.astype(jnp.float32) * weights.reshape(assigned)[None, :],
        token_hit.astype(jnp.float32),
        precision=lax.Precision.HIGHEST,
    )
    teacher = lax.dot_general(
        combine,
        returned.astype(jnp.float32),
        (((0,), (0,)), ((), ())),
        precision=lax.Precision.HIGHEST,
    ).astype(jnp.bfloat16)

    teacher_far = swap(teacher, "c")
    pair = swap(teacher, "xl")
    order = jnp.stack([yh ^ xl, yh ^ xl ^ 1, core])
    pieces = product_pieces(order, teacher, teacher_far, pair, swap(pair, "c"), proj_block)
    pieces = [
        lax.ppermute(piece, ALL, permutation(home_target(step))).astype(jnp.float32)
        for step, piece in enumerate(pieces)
    ]
    target = pieces[0] + pieces[1]

    output_difference = student_out - target
    tokens_all = tok_rows * experts
    scale = 1.0 / math.sqrt(tokens_all)
    scaled = (output_difference * scale).astype(jnp.bfloat16)
    loss_here = jnp.sum(output_difference * output_difference)
    back_part = lax.dot_general(
        scaled, adapter_up_matrix, (((1,), (1,)), ((), ())), preferred_element_type=jnp.float32
    )
    back_low = (adapter_scale_factor * mp_sum(back_part)).astype(jnp.bfloat16)
    over_tokens = (((0,), (0,)), ((), ()))
    up_part = adapter_scale_factor * lax.dot_general(
        lowrank, scaled, over_tokens, preferred_element_type=jnp.float32
    )
    down_part = lax.dot_general(back_low, normed, over_tokens, preferred_element_type=jnp.float32)

    lanes = 128
    columns = up_part.shape[1]
    tiles = rank // 8 * (columns // lanes)
    first = lax.reduce_precision(loss_here, 8, 7)
    second = lax.reduce_precision(loss_here - first, 8, 7)
    third = loss_here - first - second
    lane = jnp.arange(lanes)
    loss_row = jnp.where(
        lane == 0, first, jnp.where(lane == 1, second, jnp.where(lane == 2, third, 0.0))
    )

    def to_tiles(value):
        value = value.astype(jnp.bfloat16).reshape(rank // 8, 8, columns // lanes, lanes)
        return value.transpose(0, 2, 1, 3).reshape(tiles, 8, lanes)

    def from_tiles(value):
        value = value.reshape(rank // 8, columns // lanes, 8, lanes).transpose(0, 2, 1, 3)
        return value.reshape(rank, columns).astype(jnp.float32)

    bundle = jnp.concatenate([to_tiles(up_part), to_tiles(down_part)])
    bundle = jnp.concatenate(
        [
            bundle[: 2 * experts].reshape(experts, 16, lanes),
            bundle[2 * experts :].reshape(experts, 4, lanes),
            jnp.broadcast_to(loss_row.astype(jnp.bfloat16), (experts, 4, lanes)),
        ],
        axis=1,
    )
    bundle = lax.all_to_all(bundle, DP, split_axis=0, concat_axis=0, tiled=True)
    summed = jnp.sum(bundle.astype(jnp.float32), axis=0)
    grads = jnp.broadcast_to(summed.astype(jnp.bfloat16), (experts, 24, lanes))
    grads = lax.all_to_all(grads, DP, split_axis=0, concat_axis=0, tiled=True)
    loss = jnp.sum(mp_sum(summed[20:21])) / (tokens_all * student_width)
    grads = jnp.concatenate(
        [
            grads[:, :16].reshape(2 * experts, 8, lanes),
            grads[:, 16:20].reshape(experts // 2, 8, lanes),
        ]
    )
    up_matrix_gradient = from_tiles(grads[:tiles])
    grad_a = from_tiles(grads[tiles:]).T
    return (target, grad_a, up_matrix_gradient, loss)


def solution(mesh):
    fine = Mesh(mesh.devices.reshape(SIZES), ALL)
    placed = (
        P(DP, MP),
        P(DP, None),
        P(DP, None),
        P(DP, None, MP),
        P(DP, None, MP),
        P(DP, MP, None),
        P(DP, MP),
        P(DP, MP),
        P(MP),
        P(MP, None),
        P(None, MP),
    )
    return jax.shard_map(
        body,
        mesh=fine,
        in_specs=placed,
        out_specs=(P(DP, MP), P(MP, None), P(None, MP), P()),
        check_vma=False,
    )
```

```python
import functools
import itertools
import math

import jax
import jax.numpy as jnp
from jax import lax
from jax.experimental import pallas as pl
from jax.experimental.pallas import tpu as pltpu
from jax.sharding import Mesh, PartitionSpec as P

route_scale = 2.5
adapter_scale_factor = 0.25
DP = ("yl", "z", "xh", "xl")
MP = ("yh", "c")
ALL = DP + MP
SIZES = (2, 8, 2, 2, 2, 2)


def permutation(target):
    places = list(itertools.product(*(range(size) for size in SIZES)))
    return [(place, places.index(target(*here))) for place, here in enumerate(places)]


def proj_target(step):
    return lambda yl, z, xh, xl, yh, c: (xl ^ step, z, xh, yh, yl, c)


def home_target(step):
    return lambda yl, z, xh, xl, yh, c: (yl, z, xh, yh ^ step, xl, c)


def swap(value, axis):
    return lax.ppermute(value, axis, [(0, 1), (1, 0)])


def dot(a, b):
    return jnp.dot(a, b, preferred_element_type=jnp.float32)


def mp_sum(value):
    cross = lax.ppermute(value, MP, [(place, 3 - place) for place in range(4)])
    return (value + swap(value, "c")) + (swap(value, "yh") + cross)


def ordered(first, second, index):
    return jnp.where(
        index == 0, jnp.concatenate([first, second]), jnp.concatenate([second, first])
    )


def exchange_slots(rows):
    count, width = rows.shape
    rows = rows.reshape(64, count * width // (64 * 128), 128)
    return lax.all_to_all(rows, DP, split_axis=0, concat_axis=0, tiled=True).reshape(count, width)


def product_kernel(order_ref, own_ref, own_far_ref, pair_ref, pair_far_ref, block_ref, *refs):
    outs, near_rows, far_rows, total = refs[:2], *refs[2:]
    rows, width = own_ref.shape
    near_rows[:rows] = own_ref[...]
    near_rows[rows:] = pair_ref[...]
    far_rows[:rows] = own_far_ref[...]
    far_rows[rows:] = pair_far_ref[...]
    core = order_ref[2]
    near = pl.ds(pl.multiple_of(core * width, 128), width)
    far = pl.ds(pl.multiple_of((1 - core) * width, 128), width)
    cut = total.shape[1]
    for start in range(0, block_ref.shape[1], cut):
        columns = slice(start, start + cut)
        total[...] = dot(near_rows[...], block_ref[near, columns]) + dot(
            far_rows[...], block_ref[far, columns]
        )
        for step in range(2):
            here = pl.ds(pl.multiple_of(order_ref[step] * rows, 128), rows)
            outs[step][:, columns] = total[here, :].astype(jnp.bfloat16)


def product_pieces(order, own, own_far, pair, pair_far, block):
    rows, width = own.shape
    depth, wide = block.shape
    vmem = pl.BlockSpec(memory_space=pltpu.VMEM)
    return pl.pallas_call(
        product_kernel,
        out_shape=[jax.ShapeDtypeStruct((rows, wide), jnp.bfloat16)] * 2,
        in_specs=[pl.BlockSpec(memory_space=pltpu.SMEM)] + [vmem] * 5,
        out_specs=[vmem] * 2,
        scratch_shapes=[
            pltpu.VMEM((2 * rows, width), jnp.bfloat16),
            pltpu.VMEM((2 * rows, width), jnp.bfloat16),
            pltpu.VMEM((2 * rows, 640), jnp.float32),
        ],
        compiler_params=pltpu.CompilerParams(vmem_limit_bytes=24 * 1024 * 1024),
        cost_estimate=pl.CostEstimate(flops=100, bytes_accessed=100, transcendentals=0),
    )(order, own, own_far, pair, pair_far, block)


def stats_kernel(student_ref, gain_ref, down_ref, out_ref):
    student = student_ref[...].astype(jnp.float32)
    scaled = (student * gain_ref[...].astype(jnp.float32)).astype(jnp.bfloat16)
    rank = down_ref.shape[0]
    out_ref[:, :rank] = lax.dot_general(
        scaled, down_ref[...], (((1,), (1,)), ((), ())), preferred_element_type=jnp.float32
    )
    total = jnp.sum(student * student, axis=-1, keepdims=True)
    out_ref[:, rank:] = jnp.broadcast_to(total, (student.shape[0], rank))


def student_kernel(width, stats_ref, student_ref, gain_ref, up_ref, low_ref, normed_ref, out_ref):
    rank = up_ref.shape[0]
    inverse = lax.rsqrt(stats_ref[:, rank : rank + 1] / width + 1e-06)
    low = (stats_ref[:, :rank] * inverse).astype(jnp.bfloat16)
    student = student_ref[...].astype(jnp.float32)
    low_ref[...] = low
    normed_ref[...] = (student * inverse * gain_ref[...].astype(jnp.float32)).astype(jnp.bfloat16)
    out_ref[...] = student + adapter_scale_factor * dot(low, up_ref[...])


def home_kernel(
    scale, first_ref, second_ref, student_ref, low_ref, up_ref, target_ref, back_ref, grad_ref, loss_ref
):
    target = first_ref[...].astype(jnp.float32) + second_ref[...].astype(jnp.float32)
    target_ref[...] = target
    diff = student_ref[...] - target
    scaled = (diff * scale).astype(jnp.bfloat16)
    back_ref[...] = lax.dot_general(
        scaled, up_ref[...], (((1,), (1,)), ((), ())), preferred_element_type=jnp.float32
    )
    grad_ref[...] = adapter_scale_factor * lax.dot_general(
        low_ref[...], scaled, (((0,), (0,)), ((), ())), preferred_element_type=jnp.float32
    )
    total = jnp.sum(jnp.sum(diff * diff, axis=0, keepdims=True), axis=1, keepdims=True)
    loss_ref[...] = jnp.broadcast_to(total, loss_ref.shape)


def bundle_kernel(own_ref, core_ref, far_ref, cross_ref, normed_ref, grad_ref, loss_ref, out_ref, down_ref):
    back = (own_ref[...] + core_ref[...]) + (far_ref[...] + cross_ref[...])
    down_ref[...] = lax.dot_general(
        (adapter_scale_factor * back).astype(jnp.bfloat16),
        normed_ref[...],
        (((0,), (0,)), ((), ())),
        preferred_element_type=jnp.float32,
    )
    total = loss_ref[...]
    lane = lax.broadcasted_iota(jnp.int32, total.shape, 1)
    row = lax.broadcasted_iota(jnp.int32, total.shape, 0)
    first = total.astype(jnp.bfloat16).astype(jnp.float32)
    second = (total - first).astype(jnp.bfloat16).astype(jnp.float32)
    third = total - first - second
    loss = jnp.where(
        lane == 0, first, jnp.where(lane == 1, second, jnp.where(lane == 2, third, 0.0))
    )
    across = down_ref.shape[1] // 128
    tiles = down_ref.shape[0] // 8 * across

    def tile(number):
        ref = grad_ref if number < tiles else down_ref
        high, wide = divmod(number % tiles, across)
        return ref[high * 8 : high * 8 + 8, wide * 128 : wide * 128 + 128]

    count = out_ref.shape[0]
    for index in range(count):
        half = tile(2 * count + index // 2)
        if index % 2:
            half = pltpu.roll(half, 4, 0)
        last = jnp.where(row < 4, half, loss)
        whole = jnp.concatenate([tile(2 * index), tile(2 * index + 1), last])
        out_ref[index] = whole.astype(jnp.bfloat16)


def local_kernel(kernel, shapes, *args, scratch=()):
    vmem = pl.BlockSpec(memory_space=pltpu.VMEM)
    return pl.pallas_call(
        kernel,
        out_shape=shapes,
        in_specs=[vmem] * len(args),
        out_specs=jax.tree.map(lambda _: vmem, shapes),
        scratch_shapes=scratch,
        compiler_params=pltpu.CompilerParams(vmem_limit_bytes=16 * 1024 * 1024),
        cost_estimate=pl.CostEstimate(flops=100, bytes_accessed=100, transcendentals=0),
    )(*args)


def half_rows(ref, half, core, width):
    start = half * 2 * width
    own = pl.ds(pl.multiple_of(start + core * width, 128), width)
    other = pl.ds(pl.multiple_of(start + (1 - core) * width, 128), width)
    return ref[own, :], ref[other, :]


def near_kernel(place_ref, own_ref, other_ref, gate_ref, up_ref, down_ref, *outs):
    for out_ref, weight_ref in zip(outs, (gate_ref, up_ref)):
        own, other = half_rows(weight_ref, place_ref[0], place_ref[1], own_ref.shape[1])
        out_ref[...] = dot(own_ref[...], own) + dot(other_ref[...], other)


def expert_kernel(
    place_ref, gate_near_ref, up_near_ref, own_ref, other_ref, gate_ref, up_ref, down_ref, *outs
):
    yh, core, width = place_ref[0], place_ref[1], own_ref.shape[1]
    sums = []
    for near, weight_ref in ((gate_near_ref, gate_ref), (up_near_ref, up_ref)):
        own, other = half_rows(weight_ref, 1 - yh, core, width)
        sums.append(near[...] + dot(own_ref[...], own) + dot(other_ref[...], other))
    gate, up = sums
    hidden = (gate / (1.0 + jnp.exp(-gate)) * up).astype(jnp.bfloat16)
    parts = (yh * 2 + core, yh * 2 + 1 - core, (1 - yh) * 2 + core, (1 - yh) * 2 + 1 - core)
    for out_ref, part in zip(outs, parts):
        columns = pl.ds(pl.multiple_of(part * width, 128), width)
        out_ref[...] = dot(hidden, down_ref[:, columns]).astype(jnp.bfloat16)


def expert_call(kernel, shapes, place, *args):
    vmem = pl.BlockSpec(memory_space=pltpu.VMEM)
    return pl.pallas_call(
        kernel,
        out_shape=shapes,
        in_specs=[pl.BlockSpec(memory_space=pltpu.SMEM)] + [vmem] * len(args),
        out_specs=[vmem] * len(shapes),
        compiler_params=pltpu.CompilerParams(vmem_limit_bytes=32 * 1024 * 1024),
        cost_estimate=pl.CostEstimate(flops=100, bytes_accessed=100, transcendentals=0),
    )(place, *args)


def body(
    tokens,
    routes,
    expert_gate_affinity,
    expert_gate_weight,
    expert_up_weight,
    expert_down_weight,
    proj,
    student_hidden_input,
    student_norm_weight,
    adapter_down_matrix,
    adapter_up_matrix,
):
    experts = 64
    mp_count = 4
    tok_rows, part_width = tokens.shape
    topk_count = routes.shape[1]
    assigned = tok_rows * topk_count
    capacity = 5
    slot_count = experts * capacity
    rank = adapter_up_matrix.shape[0]
    yl, xh, xl, yh, core = (lax.axis_index(name) for name in ("yl", "xh", "xl", "yh", "c"))
    mi = yh * 2 + core

    flat_routes = routes.reshape(assigned)
    onehot_e = (flat_routes[:, None] == jnp.arange(experts, dtype=jnp.int32)[None, :]).astype(
        jnp.int32
    )
    position = jnp.sum((jnp.cumsum(onehot_e, axis=0) - onehot_e) * onehot_e, axis=1)
    slot_index = flat_routes * capacity + position
    slot_hit = (jnp.arange(slot_count, dtype=jnp.int32)[:, None] == slot_index[None, :]).astype(
        jnp.bfloat16
    )
    token_hit = (
        jnp.arange(assigned, dtype=jnp.int32)[:, None] // topk_count
        == jnp.arange(tok_rows, dtype=jnp.int32)[None, :]
    ).astype(jnp.bfloat16)
    placing = dot(slot_hit, token_hit).astype(jnp.bfloat16)
    outgoing = dot(placing, tokens).astype(jnp.bfloat16)

    outgoing, proj = lax.optimization_barrier((outgoing, proj))
    arrived = exchange_slots(outgoing)

    blocks = [lax.ppermute(proj, ALL, permutation(proj_target(step))) for step in range(2)]
    proj_rows = ordered(*blocks, yl)
    proj_rows = ordered(proj_rows, swap(proj_rows, "xh"), xh)
    arrived, proj_rows = lax.optimization_barrier((arrived, proj_rows))
    proj_block = lax.all_gather(proj_rows, "z", axis=0, tiled=True)

    arrived_y = swap(arrived, "yh")
    arrived_c = swap(arrived, "c")

    gain = student_norm_weight.reshape(1, -1)
    stats = local_kernel(
        stats_kernel,
        jax.ShapeDtypeStruct((tok_rows, 2 * rank), jnp.float32),
        student_hidden_input,
        gain,
        adapter_down_matrix.T,
    )
    stats = stats + swap(stats, "c")
    place = jnp.stack([yh, core])
    expert_weights = (expert_gate_weight[0], expert_up_weight[0], expert_down_weight[0])
    units = expert_weights[0].shape[1]
    near_gate, near_up = expert_call(
        near_kernel,
        [jax.ShapeDtypeStruct((slot_count, units), jnp.float32)] * 2,
        place,
        arrived,
        arrived_c,
        *expert_weights,
    )
    arrived_y, stats, near_gate, near_up = lax.optimization_barrier(
        (arrived_y, stats, near_gate, near_up)
    )
    out_own, out_near, out_far, out_far_near = expert_call(
        expert_kernel,
        [jax.ShapeDtypeStruct(arrived.shape, jnp.bfloat16)] * 4,
        place,
        near_gate,
        near_up,
        arrived_y,
        swap(arrived_y, "c"),
        *expert_weights,
    )
    far = swap(out_far_near, "c")
    near = swap(out_near, "c")
    far = swap((out_far.astype(jnp.float32) + far.astype(jnp.float32)).astype(jnp.bfloat16), "yh")
    expert_out = (
        out_own.astype(jnp.float32)
        + near.astype(jnp.float32)
        + far.astype(jnp.float32)
    ).astype(jnp.bfloat16)
    returned = exchange_slots(expert_out)

    stats = stats + swap(stats, "yh")
    student_width = student_hidden_input.shape[1] * mp_count
    lowrank, normed, student_out = local_kernel(
        functools.partial(student_kernel, student_width),
        [
            jax.ShapeDtypeStruct((tok_rows, rank), jnp.bfloat16),
            jax.ShapeDtypeStruct(student_hidden_input.shape, jnp.bfloat16),
            jax.ShapeDtypeStruct(student_hidden_input.shape, jnp.float32),
        ],
        stats,
        student_hidden_input,
        gain,
        adapter_up_matrix,
    )
    returned, lowrank, normed, student_out, proj_block = lax.optimization_barrier(
        (returned, lowrank, normed, student_out, proj_block)
    )

    weights = (
        route_scale * expert_gate_affinity / jnp.sum(expert_gate_affinity, axis=-1, keepdims=True)
    )
    combine = jnp.dot(
        slot_hit.astype(jnp.float32) * weights.reshape(assigned)[None, :],
        token_hit.astype(jnp.float32),
        precision=lax.Precision.HIGHEST,
    )
    teacher = lax.dot_general(
        combine,
        returned.astype(jnp.float32),
        (((0,), (0,)), ((), ())),
        precision=lax.Precision.HIGHEST,
    ).astype(jnp.bfloat16)

    teacher_far = swap(teacher, "c")
    pair = swap(teacher, "xl")
    order = jnp.stack([yh ^ xl, yh ^ xl ^ 1, core])
    pieces = product_pieces(order, teacher, teacher_far, pair, swap(pair, "c"), proj_block)
    pieces = [
        lax.ppermute(piece, ALL, permutation(home_target(step)))
        for step, piece in enumerate(pieces)
    ]
    tokens_all = tok_rows * experts
    columns = adapter_up_matrix.shape[1]
    target, back, up_part, loss_here = local_kernel(
        functools.partial(home_kernel, 1.0 / math.sqrt(tokens_all)),
        [
            jax.ShapeDtypeStruct((tok_rows, columns), jnp.float32),
            jax.ShapeDtypeStruct((tok_rows, rank), jnp.float32),
            jax.ShapeDtypeStruct((rank, columns), jnp.float32),
            jax.ShapeDtypeStruct((8, 128), jnp.float32),
        ],
        *pieces,
        student_out,
        lowrank,
        adapter_up_matrix,
    )

    lanes = 128
    tiles = rank // 8 * (columns // lanes)
    cross = [(place, 3 - place) for place in range(4)]
    bundle = local_kernel(
        bundle_kernel,
        jax.ShapeDtypeStruct((experts, 24, lanes), jnp.bfloat16),
        back,
        swap(back, "c"),
        swap(back, "yh"),
        lax.ppermute(back, MP, cross),
        normed,
        up_part,
        loss_here,
        scratch=[pltpu.VMEM((rank, columns), jnp.float32)],
    )

    def from_tiles(value):
        value = value.reshape(rank // 8, columns // lanes, 8, lanes).transpose(0, 2, 1, 3)
        return value.reshape(rank, columns).astype(jnp.float32)

    bundle = lax.all_to_all(bundle, DP, split_axis=0, concat_axis=0, tiled=True)
    summed = jnp.sum(bundle.astype(jnp.float32), axis=0)
    grads = jnp.broadcast_to(summed.astype(jnp.bfloat16), (experts, 24, lanes))
    grads = lax.all_to_all(grads, DP, split_axis=0, concat_axis=0, tiled=True)
    loss = jnp.sum(mp_sum(summed[20:21])) / (tokens_all * student_width)
    grads = jnp.concatenate(
        [
            grads[:, :16].reshape(2 * experts, 8, lanes),
            grads[:, 16:20].reshape(experts // 2, 8, lanes),
        ]
    )
    up_matrix_gradient = from_tiles(grads[:tiles])
    grad_a = from_tiles(grads[tiles:]).T
    return (target, grad_a, up_matrix_gradient, loss)


def solution(mesh):
    fine = Mesh(mesh.devices.reshape(SIZES), ALL)
    placed = (
        P(DP, MP),
        P(DP, None),
        P(DP, None),
        P(DP, None, MP),
        P(DP, None, MP),
        P(DP, MP, None),
        P(DP, MP),
        P(DP, MP),
        P(MP),
        P(MP, None),
        P(None, MP),
    )
    return jax.shard_map(
        body,
        mesh=fine,
        in_specs=placed,
        out_specs=(P(DP, MP), P(MP, None), P(None, MP), P()),
        check_vma=False,
    )
```

```python
import functools
import itertools
import math

import jax
import jax.numpy as jnp
from jax import lax
from jax.experimental import pallas as pl
from jax.experimental.pallas import tpu as pltpu
from jax.sharding import Mesh, PartitionSpec as P

route_scale = 2.5
adapter_scale_factor = 0.25
DP = ("yl", "z", "xh", "xl")
MP = ("yh", "c")
ALL = DP + MP
SIZES = (2, 8, 2, 2, 2, 2)


def permutation(target):
    places = list(itertools.product(*(range(size) for size in SIZES)))
    return [(place, places.index(target(*here))) for place, here in enumerate(places)]


def proj_target(yl, z, xh, xl, yh, c):
    return (xl, z, xh, yh, yl, c)


def home_target(step):
    return lambda yl, z, xh, xl, yh, c: (yl, z, xh, yh ^ step, xl, c)


def swap(value, axis):
    return lax.ppermute(value, axis, [(0, 1), (1, 0)])


def dot(a, b):
    return jnp.dot(a, b, preferred_element_type=jnp.float32)


def mp_sum(value):
    cross = lax.ppermute(value, MP, [(place, 3 - place) for place in range(4)])
    return (value + swap(value, "c")) + (swap(value, "yh") + cross)


def ordered(first, second, index):
    return jnp.where(
        index == 0, jnp.concatenate([first, second]), jnp.concatenate([second, first])
    )


def exchange_slots(rows):
    count, width = rows.shape
    rows = rows.reshape(64, count * width // (64 * 128), 128)
    return lax.all_to_all(rows, DP, split_axis=0, concat_axis=0, tiled=True).reshape(count, width)


def product_kernel(order_ref, own_ref, own_far_ref, pair_ref, pair_far_ref, block_ref, *refs):
    outs, near_rows, far_rows, total = refs[:2], *refs[2:]
    rows, width = own_ref.shape
    near_rows[:rows] = own_ref[...]
    near_rows[rows:] = pair_ref[...]
    far_rows[:rows] = own_far_ref[...]
    far_rows[rows:] = pair_far_ref[...]
    core = order_ref[2]
    near = pl.ds(pl.multiple_of(core * width, 128), width)
    far = pl.ds(pl.multiple_of((1 - core) * width, 128), width)
    cut = total.shape[1]
    for start in range(0, block_ref.shape[1], cut):
        columns = slice(start, start + cut)
        total[...] = dot(near_rows[...], block_ref[near, columns]) + dot(
            far_rows[...], block_ref[far, columns]
        )
        for step in range(2):
            here = pl.ds(pl.multiple_of(order_ref[step] * rows, 128), rows)
            outs[step][:, columns] = total[here, :].astype(jnp.bfloat16)


def product_pieces(order, own, own_far, pair, pair_far, block):
    rows, width = own.shape
    depth, wide = block.shape
    vmem = pl.BlockSpec(memory_space=pltpu.VMEM)
    return pl.pallas_call(
        product_kernel,
        out_shape=[jax.ShapeDtypeStruct((rows, wide), jnp.bfloat16)] * 2,
        in_specs=[pl.BlockSpec(memory_space=pltpu.SMEM)] + [vmem] * 5,
        out_specs=[vmem] * 2,
        scratch_shapes=[
            pltpu.VMEM((2 * rows, width), jnp.bfloat16),
            pltpu.VMEM((2 * rows, width), jnp.bfloat16),
            pltpu.VMEM((2 * rows, 640), jnp.float32),
        ],
        compiler_params=pltpu.CompilerParams(vmem_limit_bytes=24 * 1024 * 1024),
        cost_estimate=pl.CostEstimate(flops=100, bytes_accessed=100, transcendentals=0),
    )(order, own, own_far, pair, pair_far, block)


def stats_kernel(student_ref, gain_ref, down_ref, out_ref):
    student = student_ref[...].astype(jnp.float32)
    scaled = (student * gain_ref[...].astype(jnp.float32)).astype(jnp.bfloat16)
    rank = down_ref.shape[0]
    out_ref[:, :rank] = lax.dot_general(
        scaled, down_ref[...], (((1,), (1,)), ((), ())), preferred_element_type=jnp.float32
    )
    total = jnp.sum(student * student, axis=-1, keepdims=True)
    out_ref[:, rank:] = jnp.broadcast_to(total, (student.shape[0], rank))


def student_kernel(width, stats_ref, student_ref, gain_ref, up_ref, low_ref, normed_ref, out_ref):
    rank = up_ref.shape[0]
    inverse = lax.rsqrt(stats_ref[:, rank : rank + 1] / width + 1e-06)
    low = (stats_ref[:, :rank] * inverse).astype(jnp.bfloat16)
    student = student_ref[...].astype(jnp.float32)
    low_ref[...] = low
    normed_ref[...] = (student * inverse * gain_ref[...].astype(jnp.float32)).astype(jnp.bfloat16)
    out_ref[...] = student + adapter_scale_factor * dot(low, up_ref[...])


def home_kernel(
    scale, first_ref, second_ref, student_ref, low_ref, up_ref, target_ref, back_ref, grad_ref, loss_ref
):
    target = first_ref[...].astype(jnp.float32) + second_ref[...].astype(jnp.float32)
    target_ref[...] = target
    diff = student_ref[...] - target
    scaled = (diff * scale).astype(jnp.bfloat16)
    back_ref[...] = lax.dot_general(
        scaled, up_ref[...], (((1,), (1,)), ((), ())), preferred_element_type=jnp.float32
    )
    grad_ref[...] = adapter_scale_factor * lax.dot_general(
        low_ref[...], scaled, (((0,), (0,)), ((), ())), preferred_element_type=jnp.float32
    )
    total = jnp.sum(jnp.sum(diff * diff, axis=0, keepdims=True), axis=1, keepdims=True)
    loss_ref[...] = jnp.broadcast_to(total, loss_ref.shape)


def bundle_kernel(own_ref, core_ref, far_ref, cross_ref, normed_ref, grad_ref, loss_ref, out_ref, down_ref):
    back = (own_ref[...] + core_ref[...]) + (far_ref[...] + cross_ref[...])
    down_ref[...] = lax.dot_general(
        (adapter_scale_factor * back).astype(jnp.bfloat16),
        normed_ref[...],
        (((0,), (0,)), ((), ())),
        preferred_element_type=jnp.float32,
    )
    total = loss_ref[...]
    lane = lax.broadcasted_iota(jnp.int32, total.shape, 1)
    row = lax.broadcasted_iota(jnp.int32, total.shape, 0)
    first = total.astype(jnp.bfloat16).astype(jnp.float32)
    second = (total - first).astype(jnp.bfloat16).astype(jnp.float32)
    third = total - first - second
    loss = jnp.where(
        lane == 0, first, jnp.where(lane == 1, second, jnp.where(lane == 2, third, 0.0))
    )
    across = down_ref.shape[1] // 128
    tiles = down_ref.shape[0] // 8 * across

    def tile(number):
        ref = grad_ref if number < tiles else down_ref
        high, wide = divmod(number % tiles, across)
        return ref[high * 8 : high * 8 + 8, wide * 128 : wide * 128 + 128]

    count = out_ref.shape[0]
    for index in range(count):
        half = tile(2 * count + index // 2)
        if index % 2:
            half = pltpu.roll(half, 4, 0)
        last = jnp.where(row < 4, half, loss)
        whole = jnp.concatenate([tile(2 * index), tile(2 * index + 1), last])
        out_ref[index] = whole.astype(jnp.bfloat16)


def local_kernel(kernel, shapes, *args, scratch=()):
    vmem = pl.BlockSpec(memory_space=pltpu.VMEM)
    return pl.pallas_call(
        kernel,
        out_shape=shapes,
        in_specs=[vmem] * len(args),
        out_specs=jax.tree.map(lambda _: vmem, shapes),
        scratch_shapes=scratch,
        compiler_params=pltpu.CompilerParams(vmem_limit_bytes=16 * 1024 * 1024),
        cost_estimate=pl.CostEstimate(flops=100, bytes_accessed=100, transcendentals=0),
    )(*args)


def half_rows(ref, half, core, width):
    start = half * 2 * width
    own = pl.ds(pl.multiple_of(start + core * width, 128), width)
    other = pl.ds(pl.multiple_of(start + (1 - core) * width, 128), width)
    return ref[own, :], ref[other, :]


def near_kernel(place_ref, own_ref, other_ref, gate_ref, up_ref, down_ref, *outs):
    for out_ref, weight_ref in zip(outs, (gate_ref, up_ref)):
        own, other = half_rows(weight_ref, place_ref[0], place_ref[1], own_ref.shape[1])
        out_ref[...] = dot(own_ref[...], own) + dot(other_ref[...], other)


def expert_kernel(
    place_ref, gate_near_ref, up_near_ref, own_ref, other_ref, gate_ref, up_ref, down_ref, *outs
):
    yh, core, width = place_ref[0], place_ref[1], own_ref.shape[1]
    sums = []
    for near, weight_ref in ((gate_near_ref, gate_ref), (up_near_ref, up_ref)):
        own, other = half_rows(weight_ref, 1 - yh, core, width)
        sums.append(near[...] + dot(own_ref[...], own) + dot(other_ref[...], other))
    gate, up = sums
    hidden = (gate / (1.0 + jnp.exp(-gate)) * up).astype(jnp.bfloat16)
    parts = (yh * 2 + core, yh * 2 + 1 - core, (1 - yh) * 2 + core, (1 - yh) * 2 + 1 - core)
    for out_ref, part in zip(outs, parts):
        columns = pl.ds(pl.multiple_of(part * width, 128), width)
        out_ref[...] = dot(hidden, down_ref[:, columns]).astype(jnp.bfloat16)


def expert_call(kernel, shapes, place, *args):
    vmem = pl.BlockSpec(memory_space=pltpu.VMEM)
    return pl.pallas_call(
        kernel,
        out_shape=shapes,
        in_specs=[pl.BlockSpec(memory_space=pltpu.SMEM)] + [vmem] * len(args),
        out_specs=[vmem] * len(shapes),
        compiler_params=pltpu.CompilerParams(vmem_limit_bytes=32 * 1024 * 1024),
        cost_estimate=pl.CostEstimate(flops=100, bytes_accessed=100, transcendentals=0),
    )(place, *args)


def body(
    tokens,
    routes,
    expert_gate_affinity,
    expert_gate_weight,
    expert_up_weight,
    expert_down_weight,
    proj,
    student_hidden_input,
    student_norm_weight,
    adapter_down_matrix,
    adapter_up_matrix,
):
    experts = 64
    mp_count = 4
    tok_rows, part_width = tokens.shape
    topk_count = routes.shape[1]
    assigned = tok_rows * topk_count
    capacity = 5
    slot_count = experts * capacity
    rank = adapter_up_matrix.shape[0]
    yl, xh, xl, yh, core = (lax.axis_index(name) for name in ("yl", "xh", "xl", "yh", "c"))
    mi = yh * 2 + core

    flat_routes = routes.reshape(assigned)
    onehot_e = (flat_routes[:, None] == jnp.arange(experts, dtype=jnp.int32)[None, :]).astype(
        jnp.int32
    )
    position = jnp.sum((jnp.cumsum(onehot_e, axis=0) - onehot_e) * onehot_e, axis=1)
    slot_index = flat_routes * capacity + position
    slot_hit = (jnp.arange(slot_count, dtype=jnp.int32)[:, None] == slot_index[None, :]).astype(
        jnp.bfloat16
    )
    token_hit = (
        jnp.arange(assigned, dtype=jnp.int32)[:, None] // topk_count
        == jnp.arange(tok_rows, dtype=jnp.int32)[None, :]
    ).astype(jnp.bfloat16)
    placing = dot(slot_hit, token_hit).astype(jnp.bfloat16)
    outgoing = dot(placing, tokens).astype(jnp.bfloat16)

    outgoing, proj = lax.optimization_barrier((outgoing, proj))
    arrived = exchange_slots(outgoing)

    proj_rows = lax.ppermute(proj, ALL, permutation(proj_target))
    proj_rows = ordered(proj_rows, swap(proj_rows, "yl"), yl)
    arrived, proj_rows = lax.optimization_barrier((arrived, proj_rows))

    arrived_y = swap(arrived, "yh")
    arrived_c = swap(arrived, "c")
    proj_rows = ordered(proj_rows, swap(proj_rows, "xh"), xh)

    gain = student_norm_weight.reshape(1, -1)
    stats = local_kernel(
        stats_kernel,
        jax.ShapeDtypeStruct((tok_rows, 2 * rank), jnp.float32),
        student_hidden_input,
        gain,
        adapter_down_matrix.T,
    )
    stats = stats + swap(stats, "c")
    place = jnp.stack([yh, core])
    expert_weights = (expert_gate_weight[0], expert_up_weight[0], expert_down_weight[0])
    units = expert_weights[0].shape[1]
    near_gate, near_up = expert_call(
        near_kernel,
        [jax.ShapeDtypeStruct((slot_count, units), jnp.float32)] * 2,
        place,
        arrived,
        arrived_c,
        *expert_weights,
    )
    arrived_y, stats, near_gate, near_up, proj_rows = lax.optimization_barrier(
        (arrived_y, stats, near_gate, near_up, proj_rows)
    )
    proj_block = lax.all_gather(proj_rows, "z", axis=0, tiled=True)
    out_own, out_near, out_far, out_far_near = expert_call(
        expert_kernel,
        [jax.ShapeDtypeStruct(arrived.shape, jnp.bfloat16)] * 4,
        place,
        near_gate,
        near_up,
        arrived_y,
        swap(arrived_y, "c"),
        *expert_weights,
    )
    far = swap(out_far_near, "c")
    near = swap(out_near, "c")
    far = swap((out_far.astype(jnp.float32) + far.astype(jnp.float32)).astype(jnp.bfloat16), "yh")
    expert_out = (
        out_own.astype(jnp.float32)
        + near.astype(jnp.float32)
        + far.astype(jnp.float32)
    ).astype(jnp.bfloat16)
    returned = exchange_slots(expert_out)

    stats = stats + swap(stats, "yh")
    student_width = student_hidden_input.shape[1] * mp_count
    lowrank, normed, student_out = local_kernel(
        functools.partial(student_kernel, student_width),
        [
            jax.ShapeDtypeStruct((tok_rows, rank), jnp.bfloat16),
            jax.ShapeDtypeStruct(student_hidden_input.shape, jnp.bfloat16),
            jax.ShapeDtypeStruct(student_hidden_input.shape, jnp.float32),
        ],
        stats,
        student_hidden_input,
        gain,
        adapter_up_matrix,
    )
    returned, lowrank, normed, student_out, proj_block = lax.optimization_barrier(
        (returned, lowrank, normed, student_out, proj_block)
    )

    weights = (
        route_scale * expert_gate_affinity / jnp.sum(expert_gate_affinity, axis=-1, keepdims=True)
    )
    combine = jnp.dot(
        slot_hit.astype(jnp.float32) * weights.reshape(assigned)[None, :],
        token_hit.astype(jnp.float32),
        precision=lax.Precision.HIGHEST,
    )
    teacher = lax.dot_general(
        combine,
        returned.astype(jnp.float32),
        (((0,), (0,)), ((), ())),
        precision=lax.Precision.HIGHEST,
    ).astype(jnp.bfloat16)

    teacher_far = swap(teacher, "c")
    pair = swap(teacher, "xl")
    order = jnp.stack([yh ^ xl, yh ^ xl ^ 1, core])
    pieces = product_pieces(order, teacher, teacher_far, pair, swap(pair, "c"), proj_block)
    pieces = [
        lax.ppermute(piece, ALL, permutation(home_target(step)))
        for step, piece in enumerate(pieces)
    ]
    tokens_all = tok_rows * experts
    columns = adapter_up_matrix.shape[1]
    target, back, up_part, loss_here = local_kernel(
        functools.partial(home_kernel, 1.0 / math.sqrt(tokens_all)),
        [
            jax.ShapeDtypeStruct((tok_rows, columns), jnp.float32),
            jax.ShapeDtypeStruct((tok_rows, rank), jnp.float32),
            jax.ShapeDtypeStruct((rank, columns), jnp.float32),
            jax.ShapeDtypeStruct((8, 128), jnp.float32),
        ],
        *pieces,
        student_out,
        lowrank,
        adapter_up_matrix,
    )

    lanes = 128
    tiles = rank // 8 * (columns // lanes)
    cross = [(place, 3 - place) for place in range(4)]
    bundle = local_kernel(
        bundle_kernel,
        jax.ShapeDtypeStruct((experts, 24, lanes), jnp.bfloat16),
        back,
        swap(back, "c"),
        swap(back, "yh"),
        lax.ppermute(back, MP, cross),
        normed,
        up_part,
        loss_here,
        scratch=[pltpu.VMEM((rank, columns), jnp.float32)],
    )

    def from_tiles(value):
        value = value.reshape(rank // 8, columns // lanes, 8, lanes).transpose(0, 2, 1, 3)
        return value.reshape(rank, columns).astype(jnp.float32)

    bundle = lax.all_to_all(bundle, DP, split_axis=0, concat_axis=0, tiled=True)
    summed = jnp.sum(bundle.astype(jnp.float32), axis=0)
    grads = jnp.broadcast_to(summed.astype(jnp.bfloat16), (experts, 24, lanes))
    grads = lax.all_to_all(grads, DP, split_axis=0, concat_axis=0, tiled=True)
    loss = jnp.sum(mp_sum(summed[20:21])) / (tokens_all * student_width)
    grads = jnp.concatenate(
        [
            grads[:, :16].reshape(2 * experts, 8, lanes),
            grads[:, 16:20].reshape(experts // 2, 8, lanes),
        ]
    )
    up_matrix_gradient = from_tiles(grads[:tiles])
    grad_a = from_tiles(grads[tiles:]).T
    return (target, grad_a, up_matrix_gradient, loss)


def solution(mesh):
    fine = Mesh(mesh.devices.reshape(SIZES), ALL)
    placed = (
        P(DP, MP),
        P(DP, None),
        P(DP, None),
        P(DP, None, MP),
        P(DP, None, MP),
        P(DP, MP, None),
        P(DP, MP),
        P(DP, MP),
        P(MP),
        P(MP, None),
        P(None, MP),
    )
    return jax.shard_map(
        body,
        mesh=fine,
        in_specs=placed,
        out_specs=(P(DP, MP), P(MP, None), P(None, MP), P()),
        check_vma=False,
    )
```

```python
import functools
import itertools
import math

import jax
import jax.numpy as jnp
from jax import lax
from jax.experimental import pallas as pl
from jax.experimental.pallas import tpu as pltpu
from jax.sharding import Mesh, PartitionSpec as P

route_scale = 2.5
adapter_scale_factor = 0.25
DP = ("yl", "z", "xh", "xl")
MP = ("yh", "c")
ALL = DP + MP
SIZES = (2, 8, 2, 2, 2, 2)


def permutation(target):
    places = list(itertools.product(*(range(size) for size in SIZES)))
    return [(place, places.index(target(*here))) for place, here in enumerate(places)]


def proj_target(yl, z, xh, xl, yh, c):
    return (xl, z, xh, yh, yl, c)


def home_target(step):
    return lambda yl, z, xh, xl, yh, c: (yl, z, xh, yh ^ step, xl, c)


def swap(value, axis):
    return lax.ppermute(value, axis, [(0, 1), (1, 0)])


def mp_sum(value):
    value = value + swap(value, "c")
    return value + swap(value, "yh")


def dot(a, b):
    return jnp.dot(a, b, preferred_element_type=jnp.float32)


def pair_rows(value, axis, index):
    other = swap(value, axis)
    return jnp.where(
        index == 0, jnp.concatenate([value, other]), jnp.concatenate([other, value])
    )


def exchange_slots(rows):
    count, width = rows.shape
    rows = rows.reshape(64, count * width // (64 * 128), 128)
    return lax.all_to_all(rows, DP, split_axis=0, concat_axis=0, tiled=True).reshape(count, width)


def product_kernel(order_ref, own_ref, own_far_ref, pair_ref, pair_far_ref, block_ref, *refs):
    outs, near_rows, far_rows, total, held, arrived = refs[:2], *refs[2:]
    rows, width = own_ref.shape
    count, cut = held.shape[0], held.shape[2]
    copies = [
        pltpu.make_async_copy(
            block_ref.at[:, pl.ds(index * cut, cut)], held.at[index], arrived.at[index]
        )
        for index in range(count)
    ]
    for copy in copies:
        copy.start()
    near_rows[:rows] = own_ref[...]
    near_rows[rows:] = pair_ref[...]
    far_rows[:rows] = own_far_ref[...]
    far_rows[rows:] = pair_far_ref[...]
    core = order_ref[2]
    near = pl.ds(pl.multiple_of(core * width, 128), width)
    far = pl.ds(pl.multiple_of((1 - core) * width, 128), width)
    for index, copy in enumerate(copies):
        copy.wait()
        total[...] = dot(near_rows[...], held[index, near, :]) + dot(
            far_rows[...], held[index, far, :]
        )
        for step in range(2):
            here = pl.ds(pl.multiple_of(order_ref[step] * rows, 128), rows)
            outs[step][:, index * cut : (index + 1) * cut] = total[here, :].astype(jnp.bfloat16)


def product_pieces(order, own, own_far, pair, pair_far, block):
    rows, width = own.shape
    depth, wide = block.shape
    cut = 256
    vmem = pl.BlockSpec(memory_space=pltpu.VMEM)
    return pl.pallas_call(
        product_kernel,
        out_shape=[jax.ShapeDtypeStruct((rows, wide), jnp.bfloat16)] * 2,
        in_specs=[pl.BlockSpec(memory_space=pltpu.SMEM)]
        + [vmem] * 4
        + [pl.BlockSpec(memory_space=pltpu.HBM)],
        out_specs=[vmem] * 2,
        scratch_shapes=[
            pltpu.VMEM((2 * rows, width), jnp.bfloat16),
            pltpu.VMEM((2 * rows, width), jnp.bfloat16),
            pltpu.VMEM((2 * rows, cut), jnp.float32),
            pltpu.VMEM((wide // cut, depth, cut), jnp.bfloat16),
            pltpu.SemaphoreType.DMA((wide // cut,)),
        ],
        compiler_params=pltpu.CompilerParams(vmem_limit_bytes=24 * 1024 * 1024),
        cost_estimate=pl.CostEstimate(
            flops=4 * rows * depth * wide, bytes_accessed=6_000_000, transcendentals=0
        ),
    )(order, own, own_far, pair, pair_far, block)


def stats_kernel(student_ref, gain_ref, down_ref, out_ref):
    student = student_ref[...].astype(jnp.float32)
    scaled = (student * gain_ref[...].astype(jnp.float32)).astype(jnp.bfloat16)
    rank = down_ref.shape[0]
    out_ref[:, :rank] = lax.dot_general(
        scaled, down_ref[...], (((1,), (1,)), ((), ())), preferred_element_type=jnp.float32
    )
    total = jnp.sum(student * student, axis=-1, keepdims=True)
    out_ref[:, rank:] = jnp.broadcast_to(total, (student.shape[0], rank))


def student_kernel(width, stats_ref, student_ref, gain_ref, up_ref, low_ref, normed_ref, out_ref):
    rank = up_ref.shape[0]
    inverse = lax.rsqrt(stats_ref[:, rank : rank + 1] / width + 1e-06)
    low = (stats_ref[:, :rank] * inverse).astype(jnp.bfloat16)
    student = student_ref[...].astype(jnp.float32)
    low_ref[...] = low
    normed_ref[...] = (student * inverse * gain_ref[...].astype(jnp.float32)).astype(jnp.bfloat16)
    out_ref[...] = student + adapter_scale_factor * dot(low, up_ref[...])


def home_kernel(
    scale, first_ref, second_ref, student_ref, low_ref, up_ref, target_ref, back_ref, grad_ref, loss_ref
):
    target = first_ref[...].astype(jnp.float32) + second_ref[...].astype(jnp.float32)
    target_ref[...] = target
    diff = student_ref[...] - target
    scaled = (diff * scale).astype(jnp.bfloat16)
    back_ref[...] = lax.dot_general(
        scaled, up_ref[...], (((1,), (1,)), ((), ())), preferred_element_type=jnp.float32
    )
    grad_ref[...] = adapter_scale_factor * lax.dot_general(
        low_ref[...], scaled, (((0,), (0,)), ((), ())), preferred_element_type=jnp.float32
    )
    total = jnp.sum(jnp.sum(diff * diff, axis=0, keepdims=True), axis=1, keepdims=True)
    loss_ref[...] = jnp.broadcast_to(total, loss_ref.shape)


def bundle_kernel(own_ref, core_ref, far_ref, cross_ref, normed_ref, grad_ref, loss_ref, out_ref, down_ref):
    back = (own_ref[...] + core_ref[...]) + (far_ref[...] + cross_ref[...])
    down_ref[...] = lax.dot_general(
        (adapter_scale_factor * back).astype(jnp.bfloat16),
        normed_ref[...],
        (((0,), (0,)), ((), ())),
        preferred_element_type=jnp.float32,
    )
    total = loss_ref[...]
    lane = lax.broadcasted_iota(jnp.int32, total.shape, 1)
    row = lax.broadcasted_iota(jnp.int32, total.shape, 0)
    first = total.astype(jnp.bfloat16).astype(jnp.float32)
    second = (total - first).astype(jnp.bfloat16).astype(jnp.float32)
    third = total - first - second
    loss = jnp.where(
        lane == 0, first, jnp.where(lane == 1, second, jnp.where(lane == 2, third, 0.0))
    )
    across = down_ref.shape[1] // 128
    tiles = down_ref.shape[0] // 8 * across

    def tile(number):
        ref = grad_ref if number < tiles else down_ref
        high, wide = divmod(number % tiles, across)
        return ref[high * 8 : high * 8 + 8, wide * 128 : wide * 128 + 128]

    count = out_ref.shape[0]
    for index in range(count):
        half = tile(2 * count + index // 2)
        if index % 2:
            half = pltpu.roll(half, 4, 0)
        last = jnp.where(row < 4, half, loss)
        whole = jnp.concatenate([tile(2 * index), tile(2 * index + 1), last])
        out_ref[index] = whole.astype(jnp.bfloat16)


def local_kernel(kernel, shapes, *args, scratch=()):
    vmem = pl.BlockSpec(memory_space=pltpu.VMEM)
    return pl.pallas_call(
        kernel,
        out_shape=shapes,
        in_specs=[vmem] * len(args),
        out_specs=jax.tree.map(lambda _: vmem, shapes),
        scratch_shapes=scratch,
        compiler_params=pltpu.CompilerParams(vmem_limit_bytes=16 * 1024 * 1024),
        cost_estimate=pl.CostEstimate(flops=100, bytes_accessed=100, transcendentals=0),
    )(*args)


def body(
    tokens,
    routes,
    expert_gate_affinity,
    expert_gate_weight,
    expert_up_weight,
    expert_down_weight,
    proj,
    student_hidden_input,
    student_norm_weight,
    adapter_down_matrix,
    adapter_up_matrix,
):
    experts = 64
    mp_count = 4
    tok_rows, part_width = tokens.shape
    topk_count = routes.shape[1]
    assigned = tok_rows * topk_count
    capacity = 5
    slot_count = experts * capacity
    rank = adapter_up_matrix.shape[0]
    yl, xh, xl, yh, core = (lax.axis_index(name) for name in ("yl", "xh", "xl", "yh", "c"))
    mi = yh * 2 + core

    flat_routes = routes.reshape(assigned)
    onehot_e = (flat_routes[:, None] == jnp.arange(experts, dtype=jnp.int32)[None, :]).astype(
        jnp.int32
    )
    position = jnp.sum((jnp.cumsum(onehot_e, axis=0) - onehot_e) * onehot_e, axis=1)
    slot_index = flat_routes * capacity + position
    slot_hit = (jnp.arange(slot_count, dtype=jnp.int32)[:, None] == slot_index[None, :]).astype(
        jnp.bfloat16
    )
    token_hit = (
        jnp.arange(assigned, dtype=jnp.int32)[:, None] // topk_count
        == jnp.arange(tok_rows, dtype=jnp.int32)[None, :]
    ).astype(jnp.bfloat16)
    placing = dot(slot_hit, token_hit).astype(jnp.bfloat16)
    outgoing = dot(placing, tokens).astype(jnp.bfloat16)

    outgoing, proj = lax.optimization_barrier((outgoing, proj))
    arrived = exchange_slots(outgoing)

    proj_rows = lax.ppermute(proj, ALL, permutation(proj_target))
    proj_rows = pair_rows(proj_rows, "yl", yl)
    arrived, proj_rows = lax.optimization_barrier((arrived, proj_rows))

    arrived_y = swap(arrived, "yh")
    arrived_c = swap(arrived, "c")
    proj_rows = pair_rows(proj_rows, "xh", xh)

    gain = student_norm_weight.reshape(1, -1)
    stats = local_kernel(
        stats_kernel,
        jax.ShapeDtypeStruct((tok_rows, 2 * rank), jnp.float32),
        student_hidden_input,
        gain,
        adapter_down_matrix.T,
    )
    stats = stats + swap(stats, "c")
    arrived_y, proj_rows, stats = lax.optimization_barrier((arrived_y, proj_rows, stats))
    proj_block = lax.all_gather(proj_rows, "z", axis=0, tiled=True)
    arrived_yc = swap(arrived_y, "c")
    parts = (
        (arrived, mi),
        (arrived_c, yh * 2 + 1 - core),
        (arrived_y, (1 - yh) * 2 + core),
        (arrived_yc, (1 - yh) * 2 + 1 - core),
    )
    gate_proj = up_proj = 0.0
    for rows, place in parts:
        gate_proj = gate_proj + dot(
            rows, lax.dynamic_slice_in_dim(expert_gate_weight[0], place * part_width, part_width, 0)
        )
        up_proj = up_proj + dot(
            rows, lax.dynamic_slice_in_dim(expert_up_weight[0], place * part_width, part_width, 0)
        )
    hidden = (jax.nn.silu(gate_proj) * up_proj).astype(jnp.bfloat16)

    def out_part(place):
        return dot(
            hidden, lax.dynamic_slice_in_dim(expert_down_weight[0], place * part_width, part_width, 1)
        )

    far = swap(out_part((1 - yh) * 2 + 1 - core).astype(jnp.bfloat16), "c")
    near = swap(out_part(yh * 2 + 1 - core).astype(jnp.bfloat16), "c")
    far = out_part((1 - yh) * 2 + core).astype(jnp.bfloat16).astype(jnp.float32) + far.astype(
        jnp.float32
    )
    far = swap(far.astype(jnp.bfloat16), "yh")
    expert_out = (
        out_part(mi).astype(jnp.bfloat16).astype(jnp.float32)
        + near.astype(jnp.float32)
        + far.astype(jnp.float32)
    ).astype(jnp.bfloat16)
    returned = exchange_slots(expert_out)

    stats = stats + swap(stats, "yh")
    student_width = student_hidden_input.shape[1] * mp_count
    lowrank, normed, student_out = local_kernel(
        functools.partial(student_kernel, student_width),
        [
            jax.ShapeDtypeStruct((tok_rows, rank), jnp.bfloat16),
            jax.ShapeDtypeStruct(student_hidden_input.shape, jnp.bfloat16),
            jax.ShapeDtypeStruct(student_hidden_input.shape, jnp.float32),
        ],
        stats,
        student_hidden_input,
        gain,
        adapter_up_matrix,
    )
    returned, lowrank, normed, student_out = lax.optimization_barrier(
        (returned, lowrank, normed, student_out)
    )

    weights = (
        route_scale * expert_gate_affinity / jnp.sum(expert_gate_affinity, axis=-1, keepdims=True)
    )
    combine = jnp.dot(
        slot_hit.astype(jnp.float32) * weights.reshape(assigned)[None, :],
        token_hit.astype(jnp.float32),
        precision=lax.Precision.HIGHEST,
    )
    teacher = lax.dot_general(
        combine,
        returned.astype(jnp.float32),
        (((0,), (0,)), ((), ())),
        precision=lax.Precision.HIGHEST,
    ).astype(jnp.bfloat16)

    teacher_far = swap(teacher, "c")
    pair = swap(teacher, "xl")
    order = jnp.stack([yh ^ xl, yh ^ xl ^ 1, core])
    pieces = product_pieces(order, teacher, teacher_far, pair, swap(pair, "c"), proj_block)
    pieces = [
        lax.ppermute(piece, ALL, permutation(home_target(step)))
        for step, piece in enumerate(pieces)
    ]
    tokens_all = tok_rows * experts
    columns = adapter_up_matrix.shape[1]
    target, back, up_part, loss_here = local_kernel(
        functools.partial(home_kernel, 1.0 / math.sqrt(tokens_all)),
        [
            jax.ShapeDtypeStruct((tok_rows, columns), jnp.float32),
            jax.ShapeDtypeStruct((tok_rows, rank), jnp.float32),
            jax.ShapeDtypeStruct((rank, columns), jnp.float32),
            jax.ShapeDtypeStruct((8, 128), jnp.float32),
        ],
        *pieces,
        student_out,
        lowrank,
        adapter_up_matrix,
    )

    lanes = 128
    tiles = rank // 8 * (columns // lanes)
    cross = [(place, 3 - place) for place in range(4)]
    bundle = local_kernel(
        bundle_kernel,
        jax.ShapeDtypeStruct((experts, 24, lanes), jnp.bfloat16),
        back,
        swap(back, "c"),
        swap(back, "yh"),
        lax.ppermute(back, MP, cross),
        normed,
        up_part,
        loss_here,
        scratch=[pltpu.VMEM((rank, columns), jnp.float32)],
    )

    def from_tiles(value):
        value = value.reshape(rank // 8, columns // lanes, 8, lanes).transpose(0, 2, 1, 3)
        return value.reshape(rank, columns).astype(jnp.float32)

    bundle = lax.all_to_all(bundle, DP, split_axis=0, concat_axis=0, tiled=True)
    summed = jnp.sum(bundle.astype(jnp.float32), axis=0)
    grads = jnp.broadcast_to(summed.astype(jnp.bfloat16), (experts, 24, lanes))
    grads = lax.all_to_all(grads, DP, split_axis=0, concat_axis=0, tiled=True)
    loss_row = summed[20:21]
    cross = [(i, 3 - i) for i in range(4)]
    loss_row = (loss_row + swap(loss_row, "c")) + (
        swap(loss_row, "yh") + lax.ppermute(loss_row, MP, cross)
    )
    loss = jnp.sum(loss_row) / (tokens_all * student_width)
    grads = jnp.concatenate(
        [
            grads[:, :16].reshape(2 * experts, 8, lanes),
            grads[:, 16:20].reshape(experts // 2, 8, lanes),
        ]
    )
    up_matrix_gradient = from_tiles(grads[:tiles])
    grad_a = from_tiles(grads[tiles:]).T
    return (target, grad_a, up_matrix_gradient, loss)


def solution(mesh):
    fine = Mesh(mesh.devices.reshape(SIZES), ALL)
    placed = (
        P(DP, MP),
        P(DP, None),
        P(DP, None),
        P(DP, None, MP),
        P(DP, None, MP),
        P(DP, MP, None),
        P(DP, MP),
        P(DP, MP),
        P(MP),
        P(MP, None),
        P(None, MP),
    )
    return jax.shard_map(
        body,
        mesh=fine,
        in_specs=placed,
        out_specs=(P(DP, MP), P(MP, None), P(None, MP), P()),
        check_vma=False,
    )
```
